128 devices in a mesh: dp: 16 (over z_hi, x, core), tensor: 8 (over z_lo, y).
Axes of the slice: x: 4, y: 4, z: 4 (z_hi: 2, z_lo: 2; z = z_hi * 2 + z_lo), core: 2. Of those that a mesh axis runs over, the one named last changes fastest.
Arguments:
- query: bfloat16 [16384, 8192], P('dp', 'tensor'), may hold values from -17 to 17
- key_resp: bfloat16 [16384, 1024], P('dp', 'tensor'), may hold values from -4 to 4
- value_resp: bfloat16 [16384, 1024], P('dp', 'tensor'), may hold values from -4 to 4
- d_hidden: bfloat16 [16384, 5120], P('dp', 'tensor'), may hold values from -6 to 6
- w_out: bfloat16 [8192, 5120], P('tensor'), may hold values from -0.0625 to 0.0625
- prompt_key: bfloat16 [8192, 1024], P('dp', 'tensor'), may hold values from -4 to 4
- prompt_value: bfloat16 [8192, 1024], P('dp', 'tensor'), may hold values from -4 to 4
- response_group: int32 [64], P('dp'), may hold values from 0 to 15, as said below
- response_length: int32 [64], P('dp'), may hold values from 32 to 256, as said below
- prompt_owner: int32 [16], replicated, may hold values from 0 to 15, each once
Outputs:
- d_query: bfloat16 [16384, 8192], P('dp', 'tensor')
- d_key_resp: bfloat16 [16384, 1024], P('dp', 'tensor')
- d_value_resp: bfloat16 [16384, 1024], P('dp', 'tensor')
- d_prompt_key: bfloat16 [8192, 1024], P('dp', 'tensor')
- d_prompt_value: bfloat16 [8192, 1024], P('dp', 'tensor')
The draws below stay inside these ranges and needn't reach their ends.
Inputs may be any that keep to these rules, and one draw needn't show every extreme that they name: `response_group`: each group number is named by exactly 4 responses. `response_length`: the real tokens of each response; the later of its 256 slots are padding.
All inputs are finite; a program needn't handle non-finite values.
Results may differ from the reference program's by a relative error of at most 0.0067.
Values may be sent and summed in bfloat16 or wider, within the bound.
A program may use at most 192 MiB of HBM per device.

```python
import jax
import jax.numpy as jnp
from jax import lax

D = 5120
HEADS = 64
KV_HEADS = 8
HEAD_DIM = 128
PROMPT = 512
RESP_DEV = 4
RESP_LEN = 256
GROUPS = 16
TOKENS = 16384
N_DP = 16


def draw_query(key, part):
    key = jax.random.fold_in(key, 3)
    first_key = jax.random.fold_in(key, 0)
    base = jnp.clip(jax.random.normal(first_key, (TOKENS, HEADS, HEAD_DIM), jnp.float32), -4.0, 4.0)
    return base.reshape(TOKENS, HEADS * HEAD_DIM).astype(jnp.bfloat16)


def draw_prompt_key(key, part):
    key = jax.random.fold_in(key, 5)
    first_key = jax.random.fold_in(key, 0)
    base = jnp.clip(jax.random.normal(first_key, (GROUPS * PROMPT, KV_HEADS, HEAD_DIM), jnp.float32), -4.0, 4.0)
    return base.reshape(GROUPS * PROMPT, KV_HEADS * HEAD_DIM).astype(jnp.bfloat16)


def draw_response_group(key, part):
    key = jax.random.fold_in(key, 7)
    order = jax.random.permutation(key, GROUPS * RESP_DEV)
    return (order % GROUPS).astype(jnp.int32)


def draw_response_length(key, part):
    key = jax.random.fold_in(key, 9)
    lengths = jax.random.randint(key, (GROUPS * RESP_DEV,), RESP_LEN // 8, RESP_LEN + 1).astype(jnp.int32)
    lengths = lengths.at[0].set(RESP_LEN)
    lengths = lengths.at[1].set(RESP_LEN // 8)
    return lengths


def shard_levels(rng, shape, pieces, smallest, largest):
    gain = 1.0
    for position, blocks in pieces:
        draws = jax.random.uniform(jax.random.fold_in(jax.random.fold_in(rng, 6), position), (blocks,), jnp.float32, smallest / len(pieces), largest / len(pieces))
        gain = gain * jnp.repeat(jnp.exp(draws), shape[position] // blocks).reshape((-1,) + (1,) * (len(shape) - 1 - position))
    return gain


def gaussian(rng, extent, scale, most, cuts=(), kind=jnp.bfloat16):
    result = jax.random.normal(rng, extent, jnp.float32) * scale
    if len(cuts) > 0:
        result = shard_levels(rng, extent, cuts, -0.22, 0.18) * result
    return jnp.clip(result, min=-most, max=most).astype(kind)


def setup_inputs(seed: int = 0) -> dict:
    key_of = jax.random.split(jax.random.key(seed), 11)
    query = draw_query(jax.random.fold_in(key_of[10], 71), 0)
    key_resp = gaussian(key_of[1], (TOKENS, KV_HEADS * HEAD_DIM), 1.0, 4.0, ((0, 16), (1, 8)))
    value_resp = gaussian(key_of[2], (TOKENS, KV_HEADS * HEAD_DIM), 1.0, 4.0, ((0, 16), (1, 8)))
    d_hidden = gaussian(key_of[3], (TOKENS, D), 1.0, 6.0, ((0, 16), (1, 8)))
    w_out = gaussian(key_of[4], (HEADS * HEAD_DIM, D), (HEADS * HEAD_DIM) ** -0.5, 0.0625, ((0, 8),))
    prompt_key = draw_prompt_key(jax.random.fold_in(key_of[10], 71), 0)
    prompt_value = gaussian(key_of[6], (GROUPS * PROMPT, KV_HEADS * HEAD_DIM), 1.0, 4.0, ((0, 16), (1, 8)))
    response_group = draw_response_group(jax.random.fold_in(key_of[10], 71), 0)
    response_length = draw_response_length(jax.random.fold_in(key_of[10], 71), 0)
    prompt_owner = jax.random.permutation(key_of[9], GROUPS).astype(jnp.int32)
    return {"query": query, "key_resp": key_resp, "value_resp": value_resp, "d_hidden": d_hidden, "w_out": w_out, "prompt_key": prompt_key, "prompt_value": prompt_value, "response_group": response_group, "response_length": response_length, "prompt_owner": prompt_owner}


def product(form, left, right):
    return jnp.einsum(form, left.astype(jnp.float32), right.astype(jnp.float32))


def attend(queries, keys, values, grads, prompt_keys, prompt_values, score_scale):
    length = queries.shape[1]
    pre_scores = product("clkgd,cpkd->ckglp", queries, prompt_keys) * score_scale
    own_scores = product("clkgd,cmkd->ckglm", queries, keys) * score_scale
    causal = lax.broadcasted_iota(jnp.int32, (length, length), 0) >= lax.broadcasted_iota(jnp.int32, (length, length), 1)
    own_scores = jnp.where(causal, own_scores, -jnp.inf)
    row_max = jnp.maximum(jnp.max(pre_scores, -1), jnp.max(own_scores, -1))
    denom_sum = jnp.sum(jnp.exp(pre_scores - row_max[..., None]), -1) + jnp.sum(jnp.exp(own_scores - row_max[..., None]), -1)
    log_total = row_max + jnp.log(denom_sum)
    pre_probs = jnp.exp(pre_scores - log_total[..., None])
    own_probs = jnp.exp(own_scores - log_total[..., None])
    pre_round = pre_probs.astype(jnp.bfloat16)
    own_round = own_probs.astype(jnp.bfloat16)
    attn_out = product("ckglp,cpkd->clkgd", pre_round, prompt_values) + product("ckglm,cmkd->clkgd", own_round, values)
    row_delta = jnp.transpose(jnp.sum(grads.astype(jnp.float32) * attn_out, -1), (0, 2, 3, 1))
    pre_dprob = product("clkgd,cpkd->ckglp", grads, prompt_values)
    own_dprob = product("clkgd,cmkd->ckglm", grads, values)
    pre_dscore = (pre_probs * (pre_dprob - row_delta[..., None])).astype(jnp.bfloat16)
    own_dscore = (own_probs * (own_dprob - row_delta[..., None])).astype(jnp.bfloat16)
    d_query = ((product("ckglp,cpkd->clkgd", pre_dscore, prompt_keys) + product("ckglm,cmkd->clkgd", own_dscore, keys)) * score_scale).astype(jnp.bfloat16)
    d_key = (product("ckglm,clkgd->cmkd", own_dscore, queries) * score_scale).astype(jnp.bfloat16)
    d_value = product("ckglm,clkgd->cmkd", own_round, grads).astype(jnp.bfloat16)
    pre_dkey = product("ckglp,clkgd->cpkd", pre_dscore, queries) * score_scale
    pre_dvalue = product("ckglp,clkgd->cpkd", pre_round, grads)
    return d_query, d_key, d_value, pre_dkey, pre_dvalue


def reference(query, key_resp, value_resp, d_hidden, w_out, prompt_key, prompt_value, response_group, response_length, prompt_owner):
    head_ratio = HEADS // KV_HEADS
    score_scale = HEAD_DIM ** -0.5
    grad_attn = jnp.dot(d_hidden, w_out.T, preferred_element_type=jnp.float32).astype(jnp.bfloat16)
    positions = lax.broadcasted_iota(jnp.int32, (GROUPS * RESP_DEV, RESP_LEN), 1)
    valid_rows = (positions < response_length[:, None]).reshape(TOKENS, 1)
    grad_attn = jnp.where(valid_rows, grad_attn, jnp.zeros_like(grad_attn))
    head_shape = (N_DP, RESP_DEV, RESP_LEN, KV_HEADS, head_ratio, HEAD_DIM)
    kv_shape = (N_DP, RESP_DEV, RESP_LEN, KV_HEADS, HEAD_DIM)
    queries = query.reshape(head_shape)
    grads = grad_attn.reshape(head_shape)
    keys = key_resp.reshape(kv_shape)
    values = value_resp.reshape(kv_shape)
    slots = prompt_owner[response_group].reshape(N_DP, RESP_DEV).astype(jnp.int32)
    table_keys = prompt_key.reshape(GROUPS, PROMPT, KV_HEADS, HEAD_DIM)
    table_values = prompt_value.reshape(GROUPS, PROMPT, KV_HEADS, HEAD_DIM)
    slot_ids = jnp.arange(GROUPS, dtype=jnp.int32)

    def device_step(carried, inputs):
        dev_query, dev_key, dev_value, dev_grad, dev_slots = inputs
        d_query, d_key, d_value, pre_dkey, pre_dvalue = attend(dev_query, dev_key, dev_value, dev_grad, table_keys[dev_slots], table_values[dev_slots], score_scale)
        selector = (dev_slots[None, :] == slot_ids[:, None]).astype(jnp.float32)
        sum_key = carried[0] + jnp.einsum("sc,cpkd->spkd", selector, pre_dkey, precision=lax.Precision.HIGHEST)
        sum_value = carried[1] + jnp.einsum("sc,cpkd->spkd", selector, pre_dvalue, precision=lax.Precision.HIGHEST)
        return (sum_key, sum_value), (d_query, d_key, d_value)

    zero_sum = jnp.zeros((GROUPS, PROMPT, KV_HEADS, HEAD_DIM), jnp.float32)
    sums, outputs = lax.scan(device_step, (zero_sum, zero_sum), (queries, keys, values, grads, slots))
    d_query = outputs[0].reshape(TOKENS, HEADS * HEAD_DIM)
    d_key = outputs[1].reshape(TOKENS, KV_HEADS * HEAD_DIM)
    d_value = outputs[2].reshape(TOKENS, KV_HEADS * HEAD_DIM)
    d_prompt_key = sums[0].reshape(GROUPS * PROMPT, KV_HEADS * HEAD_DIM).astype(jnp.bfloat16)
    d_prompt_value = sums[1].reshape(GROUPS * PROMPT, KV_HEADS * HEAD_DIM).astype(jnp.bfloat16)
    return (d_query, d_key, d_value, d_prompt_key, d_prompt_value)
```

```python
import functools

import jax
import jax.numpy as jnp
from jax import lax
from jax.experimental import pallas as pl
from jax.experimental.pallas import tpu as pltpu
from jax.sharding import PartitionSpec as P

HEADS_DEV = 8
HD = 128
PROMPT = 512
LEN = 256
KEYS = PROMPT + LEN
RESP = 4
N_DP = 16
SHARD = 640
PIECE = PROMPT // N_DP
SCALE = HD ** (-0.5)
SCALE_LOG2E = SCALE * 1.4426950408889634
f32, bf16 = jnp.float32, jnp.bfloat16
NT = (((1,), (1,)), ((), ()))
NN = (((1,), (0,)), ((), ()))

CUT_LO, CUT_P, CUT_HI = 64, 144, 192


def dotf(a, b, dims=NN):
    return lax.dot_general(a, b, dims, preferred_element_type=f32)


def kernel(
    group_ref, length_ref, owner_ref, q_in, k_in, v_in, h_in, w_in, pk_in, pv_in,
    dq_out, dk_out, dv_out, dpk_out, dpv_out,
    dh, w, q, g, dq, ko, vo, tab, ka, va, kt, dka, dva, ctr, rbuf, fin, frec, tile, tiles, idx_v, idx_s,
    lsem, osem, d_send, d_recv, p_send, p_recv, t_send, t_recv, a_send, a_recv, f_send, f_recv,
):
    dp = lax.axis_index("dp")
    ten = lax.axis_index("tensor")
    y, zl = lax.rem(ten, 4), ten // 4
    core, x, zh = lax.rem(dp, 2), lax.rem(dp // 2, 4), dp // 8

    def at_t(z_, y_):
        return z_ * 4 + lax.rem(y_ + 4, 4)

    def at_d(zh_, x_, c_):
        return zh_ * 8 + lax.rem(x_ + 4, 4) * 2 + c_

    t_plus, t_minus, t_z = at_t(zl, y + 1), at_t(zl, y - 1), at_t(1 - zl, y)
    d_plus, d_minus = at_d(zh, x + 1, core), at_d(zh, x - 1, core)
    d_zh, d_core = at_d(1 - zh, x, core), at_d(zh, x, 1 - core)
    place, place_zh = zh * 4 + x, (1 - zh) * 4 + x

    def cols(t_):
        return pl.ds(pl.multiple_of(t_ * SHARD, 128), SHARD)

    mine = [
        pltpu.make_async_copy(h_in, dh.at[:, cols(ten)], lsem.at[0]),
        pltpu.make_async_copy(pk_in, tab.at[0, place, core], lsem.at[1]),
        pltpu.make_async_copy(pv_in, tab.at[1, place, core], lsem.at[2]),
        pltpu.make_async_copy(q_in, q, lsem.at[3]),
        pltpu.make_async_copy(k_in, ko, lsem.at[4]),
        pltpu.make_async_copy(v_in, vo, lsem.at[5]),
        pltpu.make_async_copy(w_in, w, lsem.at[6]),
    ]
    for one in mine:
        one.start()

    slots = [owner_ref[group_ref[j]] for j in range(RESP)]
    row = lax.broadcasted_iota(jnp.int32, (8, 128), 0)
    filled = jnp.full((8, 128), -100, jnp.int32)
    for j in range(RESP):
        filled = jnp.where(row == j, slots[j], filled)
    tile[...] = filled

    barrier = pltpu.get_barrier_semaphore()
    for t_ in (t_plus, t_minus, t_z):
        pl.semaphore_signal(barrier, inc=1, device_id={"tensor": t_}, device_id_type=pl.DeviceIdType.MESH)
    for k in range(1, N_DP):
        pl.semaphore_signal(
            barrier, inc=1, device_id={"dp": lax.rem(dp + k, N_DP)}, device_id_type=pl.DeviceIdType.MESH
        )
    for one in mine[:3]:
        one.wait()
    pl.semaphore_wait(barrier, 3 + N_DP - 1)

    def send(src, dst, ss, rs, axis, target):
        pltpu.make_async_remote_copy(
            src_ref=src, dst_ref=dst, send_sem=ss, recv_sem=rs, device_id={axis: target},
            device_id_type=pl.DeviceIdType.MESH,
        ).start()

    def landed(ref, sem):
        pltpu.make_async_copy(ref, ref, sem).wait()

    def far(z_, y_):
        return at_t(z_, y_)

    nz = 1 - zl
    messages = [
        (ten, far(zl, y - 1), 0, LEN, t_plus),
        (ten, far(zl, y + 1), 0, LEN, t_minus),
        (ten, t_z, 0, LEN, t_z),
        (t_z, far(nz, y - 1), 0, CUT_P, t_plus),
        (t_z, far(nz, y + 1), 0, CUT_P, t_minus),
        (t_minus, far(zl, y + 2), CUT_LO, CUT_HI, t_plus),
        (t_plus, far(zl, y + 2), 0, CUT_LO, t_minus),
        (t_plus, far(zl, y + 2), CUT_HI, LEN, t_minus),
        (t_minus, far(nz, y - 1), CUT_P, LEN, t_z),
        (t_plus, far(nz, y + 1), CUT_P, LEN, t_z),
        (far(nz, y - 1), far(nz, y + 2), CUT_LO, CUT_P, t_plus),
        (far(nz, y + 1), far(nz, y + 2), 0, CUT_LO, t_minus),
        (far(zl, y + 2), far(nz, y + 2), CUT_P, CUT_HI, t_z),
        (far(zl, y + 2), far(nz, y + 2), CUT_HI, LEN, t_z),
    ]
    steps = ((0, 3), (3, 10), (10, 14))

    def part(c, shard, lo, hi):
        return dh.at[pl.ds(pl.multiple_of(c * LEN + lo, 16), hi - lo), cols(shard)]

    def h_send(c, step):
        for m in range(*steps[step]):
            source, _, lo, hi, target = messages[m]
            block = part(c, source, lo, hi)
            send(block, block, d_send.at[c, m], d_recv.at[c, m], "tensor", target)

    def h_wait(c, step):
        for m in range(*steps[step]):
            _, got, lo, hi, _ = messages[m]
            landed(part(c, got, lo, hi), d_recv.at[c, m])

    def h_done(c):
        for m in range(len(messages)):
            source, _, lo, hi, _ = messages[m]
            landed(part(c, source, lo, hi), d_send.at[c, m])

    def pair(p_, c_):
        return tab.at[:, p_, c_]

    def spot(zh_, x_):
        return zh_ * 4 + lax.rem(x_ + 4, 4)

    nh = 1 - zh

    def line(zh_, c_):
        return tab.at[:, pl.ds(zh_ * 4, 4), c_]

    prompts = [
        (pair(place, core), pair(place_zh, core), d_zh),
        (pair(place, core), pair(spot(zh, x - 1), core), d_plus),
        (pair(place, core), pair(spot(zh, x + 1), core), d_minus),
        (pair(place_zh, core), pair(spot(nh, x - 1), core), d_plus),
        (pair(place_zh, core), pair(spot(nh, x + 1), core), d_minus),
        (tab.at[0, spot(zh, x - 1), core], tab.at[0, spot(zh, x + 2), core], d_plus),
        (tab.at[1, spot(zh, x + 1), core], tab.at[1, spot(zh, x + 2), core], d_minus),
        (tab.at[0, spot(nh, x - 1), core], tab.at[0, spot(nh, x + 2), core], d_plus),
        (tab.at[1, spot(nh, x + 1), core], tab.at[1, spot(nh, x + 2), core], d_minus),
        (line(zh, core), line(zh, 1 - core), d_core),
        (line(nh, core), line(nh, 1 - core), d_core),
    ]

    def p_go(*which):
        for m in which:
            block, _, target = prompts[m]
            send(block, block, p_send.at[m], p_recv.at[m], "dp", target)

    def p_wait(*which):
        for m in which:
            landed(prompts[m][1], p_recv.at[m])

    def spread(block, landing, ss, rs):
        for k in range(1, N_DP):
            peer = lax.rem(dp + k, N_DP)
            send(block(peer), landing, ss, rs, "dp", peer)
        pltpu.make_async_copy(block(dp), landing, rs).start()

    p_go(0, 1, 2)
    h_send(0, 0)
    for k in range(1, N_DP):
        send(tile, tiles.at[dp], t_send, t_recv, "dp", lax.rem(dp + k, N_DP))
    pltpu.make_async_copy(tile, tiles.at[dp], t_recv).start()
    h_send(1, 0)
    p_wait(1, 2)
    p_go(5, 6)
    h_wait(0, 0)
    h_send(0, 1)
    p_wait(0)
    p_go(3, 4)

    landed(tiles, t_recv)
    by_row = tiles[...].reshape(128, 128).astype(f32)
    by_lane = by_row.T
    i_row = lax.broadcasted_iota(jnp.int32, (128, 128), 0)
    i_lane = lax.broadcasted_iota(jnp.int32, (128, 128), 1)
    before = jnp.where((by_row == by_lane) & (i_row < i_lane), 1.0, 0.0)
    rank = jnp.sum(before, 0, keepdims=True)
    rank = jnp.broadcast_to(4.0 * by_lane[0:1] + rank, (64, 128))
    number = (lax.shift_right_logical(i_lane, 3) * RESP + (i_lane & 7)).astype(f32)
    hit = jnp.where(rank == i_row[:64].astype(f32), number[:64], 0.0)
    index = jnp.sum(hit, 1, keepdims=True)
    idx_v[...] = jnp.broadcast_to(index, (64, 128)).astype(jnp.int32)
    to_s = pltpu.make_async_copy(idx_v, idx_s, lsem.at[0])
    to_s.start()

    h_wait(1, 0)
    h_send(2, 0)
    p_wait(3, 4)
    p_go(7, 8)
    p_wait(5, 6)
    p_go(9)
    h_wait(0, 1)
    h_send(0, 2)
    h_send(1, 1)
    p_wait(7, 8)
    p_go(10)
    for one in mine[3:]:
        one.wait()
    p_wait(9, 10)

    HPI = 4
    WIDE = HPI * LEN
    key_at = lax.broadcasted_iota(jnp.int32, (LEN, WIDE), 0)
    row_at = lax.rem(lax.broadcasted_iota(jnp.int32, (LEN, WIDE), 1), LEN)
    causal = key_at <= row_at
    t_at = lax.broadcasted_iota(jnp.int32, (LEN, LEN), 0)

    @pl.loop(0, RESP)
    def _(c):
        rows = pl.ds(pl.multiple_of(c * LEN, LEN), LEN)
        h_wait(c, 2)

        @pl.when(c <= 1)
        def _():
            h_wait(c + 2, 0)

        @pl.when(c == 0)
        def _():
            h_send(3, 0)

        length = length_ref[c]
        slot = owner_ref[group_ref[c]]
        spot_slot = lax.shift_right_logical(slot, 1) & 7
        ka[0:PROMPT] = tab[0, spot_slot, slot & 1]
        va[0:PROMPT] = tab[1, spot_slot, slot & 1]
        ka[PROMPT:KEYS] = ko[rows]
        va[PROMPT:KEYS] = vo[rows]
        kt[...] = ka[...].astype(f32).T.astype(bf16)
        dka[...] = jnp.zeros_like(dka)
        dva[...] = jnp.zeros_like(dva)

        @pl.loop(0, 4)
        def _(n):
            some = pl.ds(pl.multiple_of(n * LEN, LEN), LEN)
            block = dotf(dh[rows, :], w[some, :], NT)
            g[rows, some] = jnp.where(t_at < length, block, 0.0).astype(bf16)

        @pl.loop(0, HEADS_DEV // HPI)
        def _(h):
            def head(i):
                return pl.ds(pl.multiple_of((h * HPI + i) * HD, HD), HD)

            q2 = jnp.concatenate([q[rows, head(i)] for i in range(HPI)], 0)
            g2 = jnp.concatenate([g[rows, head(i)] for i in range(HPI)], 0)
            s = dotf(ka[...], q2, NT)
            d = dotf(va[...], g2, NT)
            so = jnp.where(causal, s[PROMPT:], -jnp.inf)
            sp = s[:PROMPT]
            m = jnp.maximum(jnp.max(sp, 0, keepdims=True), jnp.max(so, 0, keepdims=True))
            ep = jnp.exp2((sp - m) * SCALE_LOG2E)
            eo = jnp.exp2((so - m) * SCALE_LOG2E)
            inv = 1.0 / (jnp.sum(ep, 0, keepdims=True) + jnp.sum(eo, 0, keepdims=True))
            p = jnp.concatenate([ep * inv, eo * inv], 0)
            pr = p.astype(bf16)
            delta = jnp.sum(pr.astype(f32) * d, 0, keepdims=True)
            ds = (p * (d - delta)).astype(bf16)
            dva[...] += dotf(pr, g2)
            dka[...] += dotf(ds, q2)
            dqt = dotf(kt[...], ds) * SCALE
            for i in range(HPI):
                dq[rows, head(i)] = dqt[:, i * LEN : (i + 1) * LEN].T.astype(bf16)

            @pl.when((h == 0) & (c <= 2))
            def _():
                h_wait(c + 1, 1)
                h_send(c + 1, 2)

            @pl.when((h == 0) & (c <= 1))
            def _():
                h_send(c + 2, 1)

        ctr[c, :, 0] = (dka[0:PROMPT] * SCALE).astype(bf16).reshape(N_DP, PIECE, HD)
        ctr[c, :, 1] = dva[0:PROMPT].astype(bf16).reshape(N_DP, PIECE, HD)
        spread(lambda k: ctr.at[c, k], rbuf.at[c, dp], a_send.at[c], a_recv.at[c])
        dk_out[rows] = (dka[PROMPT:KEYS] * SCALE).astype(bf16)
        dv_out[rows] = dva[PROMPT:KEYS].astype(bf16)
        pltpu.make_async_copy(dq.at[rows], dq_out.at[rows], osem.at[c]).start()

    to_s.wait()
    for c in range(RESP):
        landed(rbuf.at[c], a_recv.at[c])

    @pl.loop(0, N_DP)
    def _(s):
        total = jnp.zeros((2, PIECE, HD), f32)
        for k in range(RESP):
            r = idx_s[s * RESP + k, 0]
            total += rbuf[r & (RESP - 1), lax.shift_right_logical(r, 2) & (N_DP - 1)].astype(f32)
        fin[s] = total.astype(bf16)

    spread(lambda k: fin.at[k], frec.at[dp], f_send, f_recv)

    landed(tiles.at[0:15], t_send)
    for c in range(RESP):
        h_done(c)
        landed(ctr.at[c, 0:15], a_send.at[c])
        done = pl.ds(c * LEN, LEN)
        pltpu.make_async_copy(dq.at[done], dq_out.at[done], osem.at[c]).wait()
    for m, (block, _, _) in enumerate(prompts):
        landed(block, p_send.at[m])
    landed(frec, f_recv)
    landed(fin.at[0:15], f_send)
    dpk_out[...] = frec[:, 0].reshape(PROMPT, HD)
    dpv_out[...] = frec[:, 1].reshape(PROMPT, HD)


def body(q, k, v, h, w, pk, pv, group, length, owner):
    def out(a):
        return jax.ShapeDtypeStruct(a.shape, a.dtype)

    any_, vmem, smem = (pl.BlockSpec(memory_space=m) for m in (pl.ANY, pltpu.VMEM, pltpu.SMEM))
    dma = pltpu.SemaphoreType.DMA
    return pl.pallas_call(
        kernel,
        out_shape=(out(q), out(k), out(v), out(pk), out(pv)),
        in_specs=[smem] * 3 + [any_] * 7,
        out_specs=(any_, vmem, vmem, vmem, vmem),
        scratch_shapes=[
            pltpu.VMEM((RESP * LEN, 8 * SHARD), bf16),
            pltpu.VMEM((HEADS_DEV * HD, 8 * SHARD), bf16),
            pltpu.VMEM((RESP * LEN, HEADS_DEV * HD), bf16),
            pltpu.VMEM((RESP * LEN, HEADS_DEV * HD), bf16),
            pltpu.VMEM((RESP * LEN, HEADS_DEV * HD), bf16),
            pltpu.VMEM((RESP * LEN, HD), bf16),
            pltpu.VMEM((RESP * LEN, HD), bf16),
            pltpu.VMEM((2, 8, 2, PROMPT, HD), bf16),
            pltpu.VMEM((KEYS, HD), bf16),
            pltpu.VMEM((KEYS, HD), bf16),
            pltpu.VMEM((HD, KEYS), bf16),
            pltpu.VMEM((KEYS, HD), f32),
            pltpu.VMEM((KEYS, HD), f32),
            pltpu.VMEM((RESP, N_DP, 2, PIECE, HD), bf16),
            pltpu.VMEM((RESP, N_DP, 2, PIECE, HD), bf16),
            pltpu.VMEM((N_DP, 2, PIECE, HD), bf16),
            pltpu.VMEM((N_DP, 2, PIECE, HD), bf16),
            pltpu.VMEM((8, 128), jnp.int32),
            pltpu.VMEM((N_DP, 8, 128), jnp.int32),
            pltpu.VMEM((64, 128), jnp.int32),
            pltpu.SMEM((64, 128), jnp.int32),
            dma((7,)), dma((RESP,)), dma((RESP, 14)), dma((RESP, 14)), dma((11,)), dma((11,)),
            dma, dma, dma((RESP,)), dma((RESP,)), dma, dma,
        ],
        compiler_params=pltpu.CompilerParams(
            collective_id=0, has_side_effects=True, vmem_limit_bytes=60 * 2**20
        ),
        cost_estimate=pl.CostEstimate(flops=19 * 10**9, bytes_accessed=20 * 10**6, transcendentals=6 * 10**6),
        name="attention_backward",
    )(group, length, owner, q, k, v, h, w, pk, pv)


def solution(mesh):
    whole = P("dp", "tensor")
    return jax.shard_map(
        body,
        mesh=mesh,
        in_specs=(whole, whole, whole, whole, P("tensor", None), whole, whole, P("dp"), P("dp"), P()),
        out_specs=(whole,) * 5,
        check_vma=False,
    )
```

```python
import functools

import jax
import jax.numpy as jnp
from jax import lax
from jax.experimental import pallas as pl
from jax.experimental.pallas import tpu as pltpu
from jax.sharding import PartitionSpec as P

HEADS_DEV = 8
HD = 128
PROMPT = 512
LEN = 256
KEYS = PROMPT + LEN
RESP = 4
N_DP = 16
SHARD = 640
PIECE = PROMPT // N_DP
EXTRA = 16
HPI = 4
HALVES = HEADS_DEV // HPI
WIDE = HPI * LEN
SCALE = HD ** (-0.5)
SCALE_LOG2E = SCALE * 1.4426950408889634
f32, bf16 = jnp.float32, jnp.bfloat16
NT = (((1,), (1,)), ((), ()))
NN = (((1,), (0,)), ((), ()))

CUT_LO, CUT_P, CUT_HI = 80, 176, 192


def dotf(a, b, dims=NN):
    return lax.dot_general(a, b, dims, preferred_element_type=f32)


def kernel(
    group_ref, length_ref, owner_ref, q_in, k_in, v_in, h_in, w_in, pk_in, pv_in,
    dq_out, dk_out, dv_out, dpk_out, dpv_out,
    dh, w, q, g, dq, ko, vo, dko, dvo, tab, ka, va, kt, gacc, pb, prb, dsb, dka, dva, ctr, rbk, rbv, fin, frec, idx_v, idx_s,
    lsem, osem, d_send, d_recv, p_send, p_recv, a_send, a_recv, f_send, f_recv,
):
    dp = lax.axis_index("dp")
    ten = lax.axis_index("tensor")
    y, zl = lax.rem(ten, 4), ten // 4
    core, x, zh = lax.rem(dp, 2), lax.rem(dp // 2, 4), dp // 8

    def at_t(z_, y_):
        return z_ * 4 + lax.rem(y_ + 4, 4)

    def at_d(zh_, x_, c_):
        return zh_ * 8 + lax.rem(x_ + 4, 4) * 2 + c_

    t_plus, t_minus, t_z = at_t(zl, y + 1), at_t(zl, y - 1), at_t(1 - zl, y)
    d_plus, d_minus = at_d(zh, x + 1, core), at_d(zh, x - 1, core)
    d_zh, d_core = at_d(1 - zh, x, core), at_d(zh, x, 1 - core)
    place, place_zh = zh * 4 + x, (1 - zh) * 4 + x

    def cols(t_):
        return pl.ds(pl.multiple_of(t_ * SHARD, 128), SHARD)

    mine = [
        pltpu.make_async_copy(h_in, dh.at[:, cols(ten)], lsem.at[0]),
        pltpu.make_async_copy(pk_in, tab.at[0, place, core, 0:PROMPT], lsem.at[1]),
        pltpu.make_async_copy(pv_in, tab.at[1, place, core, 0:PROMPT], lsem.at[2]),
        pltpu.make_async_copy(q_in, q, lsem.at[3]),
        pltpu.make_async_copy(k_in, ko, lsem.at[4]),
        pltpu.make_async_copy(v_in, vo, lsem.at[5]),
        pltpu.make_async_copy(w_in, w, lsem.at[6]),
    ]
    for one in mine:
        one.start()

    slots = [owner_ref[group_ref[j]] for j in range(RESP)]
    row = lax.broadcasted_iota(jnp.int32, (EXTRA, HD), 0)
    filled = jnp.full((EXTRA, HD), -100, jnp.int32)
    for j in range(RESP):
        filled = jnp.where(row == j, slots[j], filled)
    for i in range(2):
        tab[i, place, core, PROMPT:] = filled.astype(f32).astype(bf16)

    barrier = pltpu.get_barrier_semaphore()
    for t_ in (t_plus, t_minus, t_z):
        pl.semaphore_signal(barrier, inc=1, device_id={"tensor": t_}, device_id_type=pl.DeviceIdType.MESH)
    for d_ in (d_plus, d_minus, d_zh, d_core):
        pl.semaphore_signal(barrier, inc=1, device_id={"dp": d_}, device_id_type=pl.DeviceIdType.MESH)
    for one in mine[:3]:
        one.wait()
    pl.semaphore_wait(barrier, 7)

    def send(src, dst, ss, rs, axis, target):
        pltpu.make_async_remote_copy(
            src_ref=src, dst_ref=dst, send_sem=ss, recv_sem=rs, device_id={axis: target},
            device_id_type=pl.DeviceIdType.MESH,
        ).start()

    def landed(ref, sem):
        pltpu.make_async_copy(ref, ref, sem).wait()

    def far(z_, y_):
        return at_t(z_, y_)

    nz = 1 - zl
    messages = [
        (ten, far(zl, y - 1), 0, LEN, t_plus),
        (ten, far(zl, y + 1), 0, LEN, t_minus),
        (ten, t_z, 0, LEN, t_z),
        (t_z, far(nz, y - 1), 0, CUT_P, t_plus),
        (t_z, far(nz, y + 1), 0, CUT_P, t_minus),
        (t_minus, far(zl, y + 2), CUT_LO, CUT_HI, t_plus),
        (t_plus, far(zl, y + 2), 0, CUT_LO, t_minus),
        (t_plus, far(zl, y + 2), CUT_HI, LEN, t_minus),
        (t_minus, far(nz, y - 1), CUT_P, LEN, t_z),
        (t_plus, far(nz, y + 1), CUT_P, LEN, t_z),
        (far(nz, y - 1), far(nz, y + 2), CUT_LO, CUT_P, t_plus),
        (far(nz, y + 1), far(nz, y + 2), 0, CUT_LO, t_minus),
        (far(zl, y + 2), far(nz, y + 2), CUT_P, CUT_HI, t_z),
        (far(zl, y + 2), far(nz, y + 2), CUT_HI, LEN, t_z),
    ]
    steps = ((0, 3), (3, 10), (10, 14))

    def part(c, shard, lo, hi):
        return dh.at[pl.ds(pl.multiple_of(c * LEN + lo, 16), hi - lo), cols(shard)]

    def h_send(c, step):
        for m in range(*steps[step]):
            source, _, lo, hi, target = messages[m]
            block = part(c, source, lo, hi)
            send(block, block, d_send.at[c, m], d_recv.at[c, m], "tensor", target)

    def h_wait(c, step):
        for m in range(*steps[step]):
            _, got, lo, hi, _ = messages[m]
            landed(part(c, got, lo, hi), d_recv.at[c, m])

    def h_done(c):
        for m in range(len(messages)):
            source, _, lo, hi, _ = messages[m]
            landed(part(c, source, lo, hi), d_send.at[c, m])

    def pair(p_, c_):
        return tab.at[:, p_, c_]

    def spot(zh_, x_):
        return zh_ * 4 + lax.rem(x_ + 4, 4)

    nh = 1 - zh

    def line(zh_, c_):
        return tab.at[:, pl.ds(zh_ * 4, 4), c_]

    prompts = [
        (pair(place, core), pair(place_zh, core), d_zh),
        (pair(place, core), pair(spot(zh, x - 1), core), d_plus),
        (pair(place, core), pair(spot(zh, x + 1), core), d_minus),
        (pair(place_zh, core), pair(spot(nh, x - 1), core), d_plus),
        (pair(place_zh, core), pair(spot(nh, x + 1), core), d_minus),
        (tab.at[0, spot(zh, x - 1), core], tab.at[0, spot(zh, x + 2), core], d_plus),
        (tab.at[1, spot(zh, x + 1), core], tab.at[1, spot(zh, x + 2), core], d_minus),
        (tab.at[0, spot(nh, x - 1), core], tab.at[0, spot(nh, x + 2), core], d_plus),
        (tab.at[1, spot(nh, x + 1), core], tab.at[1, spot(nh, x + 2), core], d_minus),
        (line(zh, core), line(zh, 1 - core), d_core),
        (line(nh, core), line(nh, 1 - core), d_core),
    ]

    def p_go(*which):
        for m in which:
            block, _, target = prompts[m]
            send(block, block, p_send.at[m], p_recv.at[m], "dp", target)

    def p_wait(*which):
        for m in which:
            landed(prompts[m][1], p_recv.at[m])

    def spread(block, landing, ss, rs):
        for k in range(1, N_DP):
            peer = lax.rem(dp + k, N_DP)
            send(block(peer), landing, ss, rs, "dp", peer)
        pltpu.make_async_copy(block(dp), landing, rs).start()

    p_go(0, 1, 2)
    h_send(0, 0)
    h_send(1, 0)
    p_wait(1, 2)
    p_go(5, 6)
    h_wait(0, 0)
    h_send(0, 1)
    p_wait(0)
    p_go(3, 4)

    h_wait(1, 0)
    h_send(2, 0)
    p_wait(3, 4)
    p_go(7, 8)
    p_wait(5, 6)
    p_go(9)
    h_wait(0, 1)
    h_send(0, 2)
    h_send(1, 1)
    p_wait(7, 8)
    p_go(10)
    for one in mine[3:]:
        one.wait()
    p_wait(9, 10)


    by_row = tab[0, :, :, PROMPT:].astype(f32)[:, :, 0:8].reshape(128, 128)
    by_lane = by_row.T
    i_row = lax.broadcasted_iota(jnp.int32, (128, 128), 0)
    i_lane = lax.broadcasted_iota(jnp.int32, (128, 128), 1)
    before = jnp.where((by_row == by_lane) & (i_row < i_lane), 1.0, 0.0)
    rank = jnp.sum(before, 0, keepdims=True)
    rank = jnp.broadcast_to(4.0 * by_lane[0:1] + rank, (64, 128))
    number = (lax.shift_right_logical(i_lane, 3) * RESP + (i_lane & 7)).astype(f32)
    hit = jnp.where(rank == i_row[:64].astype(f32), number[:64], 0.0)
    index = jnp.sum(hit, 1, keepdims=True)
    idx_v[...] = jnp.broadcast_to(index, (64, 128)).astype(jnp.int32)
    to_s = pltpu.make_async_copy(idx_v, idx_s, lsem.at[0])
    to_s.start()

    key_at = lax.broadcasted_iota(jnp.int32, (LEN, WIDE), 0)
    row_at = lax.rem(lax.broadcasted_iota(jnp.int32, (LEN, WIDE), 1), LEN)
    causal = key_at <= row_at
    t_at = lax.broadcasted_iota(jnp.int32, (HEADS_DEV * HD, LEN), 1)

    t_last = far(nz, y + 2)

    def gather_part(c):
        rows = pl.ds(pl.multiple_of(c * LEN, LEN), LEN)
        gacc[...] = jnp.zeros_like(gacc)

        @pl.loop(1, 8)
        def _(n):
            t_ = cols(lax.rem(t_last + n, 8))
            gacc[...] += dotf(w[:, t_], dh[rows, t_], NT)

    gather_part(0)

    def give(c, i):
        spread(lambda k: ctr.at[c, i, k], (rbk, rbv)[i].at[c, dp], a_send.at[c, i], a_recv.at[c, i])

    def add_up(i):
        for c in range(RESP):
            landed((rbk, rbv)[i].at[c], a_recv.at[c, i])

        @pl.loop(1, N_DP + 1)
        def _(n):
            s = lax.rem(dp + n, N_DP)
            total = jnp.zeros((PIECE, HD), f32)
            for k in range(RESP):
                r = idx_s[s * RESP + k, 0]
                total += (rbk, rbv)[i][r & (RESP - 1), lax.shift_right_logical(r, 2) & (N_DP - 1)].astype(f32)
            fin[i, s] = total.astype(bf16)
            landing = frec.at[i, pl.ds(dp * PIECE, PIECE)]

            @pl.when(n < N_DP)
            def _():
                send(fin.at[i, s], landing, f_send.at[i], f_recv.at[i], "dp", s)

            @pl.when(n == N_DP)
            def _():
                pltpu.make_async_copy(fin.at[i, s], landing, f_recv.at[i]).start()

    @pl.loop(0, RESP)
    def _(c):
        rows = pl.ds(pl.multiple_of(c * LEN, LEN), LEN)

        def heads(ref, h):
            return jnp.concatenate(
                [ref[rows, pl.ds(pl.multiple_of((h * HPI + i) * HD, HD), HD)] for i in range(HPI)], 0
            )

        length = length_ref[c]
        slot = owner_ref[group_ref[c]]
        spot_slot = lax.shift_right_logical(slot, 1) & 7
        ka[0:PROMPT] = tab[0, spot_slot, slot & 1, 0:PROMPT]
        va[0:PROMPT] = tab[1, spot_slot, slot & 1, 0:PROMPT]
        ka[PROMPT:KEYS] = ko[rows]
        va[PROMPT:KEYS] = vo[rows]
        kt[...] = ka[...].astype(f32).T.astype(bf16)
        dka[...] = jnp.zeros_like(dka)
        dva[...] = jnp.zeros_like(dva)

        @pl.loop(0, HALVES)
        def _(h):
            s = dotf(ka[...], heads(q, h), NT)
            so = jnp.where(causal, s[PROMPT:], -jnp.inf)
            sp = s[:PROMPT]
            m = jnp.maximum(jnp.max(sp, 0, keepdims=True), jnp.max(so, 0, keepdims=True))
            ep = jnp.exp2((sp - m) * SCALE_LOG2E)
            eo = jnp.exp2((so - m) * SCALE_LOG2E)
            inv = 1.0 / (jnp.sum(ep, 0, keepdims=True) + jnp.sum(eo, 0, keepdims=True))
            p = jnp.concatenate([ep * inv, eo * inv], 0)
            pb[h] = p
            prb[h] = p.astype(bf16)

        h_wait(c, 2)

        @pl.when(c <= 1)
        def _():
            h_wait(c + 2, 0)

        @pl.when(c == 0)
        def _():
            h_send(3, 0)

        grad = gacc[...] + dotf(w[:, cols(t_last)], dh[rows, cols(t_last)], NT)
        g[rows, :] = jnp.where(t_at < length, grad, 0.0).T.astype(bf16)

        @pl.loop(0, HALVES)
        def _(h):
            dva[...] += dotf(prb[h], heads(g, h))

        ctr[c, 1] = dva[0:PROMPT].astype(bf16).reshape(N_DP, PIECE, HD)
        give(c, 1)

        @pl.loop(0, HALVES)
        def _(h):
            d = dotf(va[...], heads(g, h), NT)
            delta = jnp.sum(prb[h].astype(f32) * d, 0, keepdims=True)
            ds = (pb[h] * (d - delta)).astype(bf16)
            dsb[h] = ds
            dka[...] += dotf(ds, heads(q, h))

        ctr[c, 0] = (dka[0:PROMPT] * SCALE).astype(bf16).reshape(N_DP, PIECE, HD)
        give(c, 0)

        @pl.when(c <= 2)
        def _():
            h_wait(c + 1, 1)
            h_send(c + 1, 2)

        @pl.when(c <= 1)
        def _():
            h_send(c + 2, 1)

        @pl.when(c <= 2)
        def _():
            gather_part(c + 1)

        @pl.when(c == RESP - 1)
        def _():
            to_s.wait()
            add_up(1)

        @pl.loop(0, HALVES)
        def _(h):
            dqt = dotf(kt[...], dsb[h]) * SCALE
            for i in range(HPI):
                head = pl.ds(pl.multiple_of((h * HPI + i) * HD, HD), HD)
                dq[rows, head] = dqt[:, i * LEN : (i + 1) * LEN].T.astype(bf16)

        dko[rows] = (dka[PROMPT:KEYS] * SCALE).astype(bf16)
        dvo[rows] = dva[PROMPT:KEYS].astype(bf16)
        for n, (block, out) in enumerate(((dq, dq_out), (dko, dk_out), (dvo, dv_out))):
            pltpu.make_async_copy(block.at[rows], out.at[rows], osem.at[c, n]).start()

    add_up(0)
    for c in range(RESP):
        h_done(c)
        for i in range(2):
            landed(ctr.at[c, i, 0:15], a_send.at[c, i])
        done = pl.ds(c * LEN, LEN)
        for n, (block, out) in enumerate(((dq, dq_out), (dko, dk_out), (dvo, dv_out))):
            pltpu.make_async_copy(block.at[done], out.at[done], osem.at[c, n]).wait()
    for m, (block, _, _) in enumerate(prompts):
        landed(block, p_send.at[m])
    last = [
        pltpu.make_async_copy(frec.at[1], dpv_out, lsem.at[1]),
        pltpu.make_async_copy(frec.at[0], dpk_out, lsem.at[2]),
    ]
    for i in (1, 0):
        landed(frec.at[i], f_recv.at[i])
        last[1 - i].start()
    for i in (1, 0):
        landed(fin.at[i, 0:15], f_send.at[i])
        last[1 - i].wait()


def hand_over(*refs):
    n = (len(refs) - 2) // 3
    sources, targets, held, sem_in, sem_out = refs[:n], refs[n : 2 * n], refs[2 * n : 3 * n], refs[-2], refs[-1]
    parts = [(i, pl.ds(k * LEN, LEN)) for i in range(n) for k in range(sources[i].shape[0] // LEN if i == 0 else 1)]
    parts = [(i, p if i == 0 else pl.ds(0, sources[i].shape[0])) for i, p in parts]
    into = [
        pltpu.make_async_copy(sources[i].at[p], held[i].at[p], sem_in.at[k]) for k, (i, p) in enumerate(parts)
    ]
    out = [
        pltpu.make_async_copy(held[i].at[p], targets[i].at[p], sem_out.at[k]) for k, (i, p) in enumerate(parts)
    ]
    for one in into:
        one.start()
    for first, second in zip(into, out):
        first.wait()
        second.start()
    for one in out:
        one.wait()


def body(q, k, v, h, w, pk, pv, group, length, owner):
    def out(a):
        return jax.ShapeDtypeStruct(a.shape, a.dtype)

    any_, smem = (pl.BlockSpec(memory_space=m) for m in (pl.ANY, pltpu.SMEM))
    dma = pltpu.SemaphoreType.DMA
    outs = (out(q), out(k), out(v), out(pk), out(pv))
    grads = pl.pallas_call(
        kernel,
        out_shape=outs,
        in_specs=[smem] * 3 + [any_] * 7,
        out_specs=(any_,) * 5,
        scratch_shapes=[
            pltpu.VMEM((RESP * LEN, 8 * SHARD), bf16),
            pltpu.VMEM((HEADS_DEV * HD, 8 * SHARD), bf16),
            pltpu.VMEM((RESP * LEN, HEADS_DEV * HD), bf16),
            pltpu.VMEM((RESP * LEN, HEADS_DEV * HD), bf16),
            pltpu.VMEM((RESP * LEN, HEADS_DEV * HD), bf16),
            pltpu.VMEM((RESP * LEN, HD), bf16),
            pltpu.VMEM((RESP * LEN, HD), bf16),
            pltpu.VMEM((RESP * LEN, HD), bf16),
            pltpu.VMEM((RESP * LEN, HD), bf16),
            pltpu.VMEM((2, 8, 2, PROMPT + EXTRA, HD), bf16),
            pltpu.VMEM((KEYS, HD), bf16),
            pltpu.VMEM((KEYS, HD), bf16),
            pltpu.VMEM((HD, KEYS), bf16),
            pltpu.VMEM((HEADS_DEV * HD, LEN), f32),
            pltpu.VMEM((HALVES, KEYS, WIDE), f32),
            pltpu.VMEM((HALVES, KEYS, WIDE), bf16),
            pltpu.VMEM((HALVES, KEYS, WIDE), bf16),
            pltpu.VMEM((KEYS, HD), f32),
            pltpu.VMEM((KEYS, HD), f32),
            pltpu.VMEM((RESP, 2, N_DP, PIECE, HD), bf16),
            pltpu.VMEM((RESP, N_DP, PIECE, HD), bf16),
            pltpu.VMEM((RESP, N_DP, PIECE, HD), bf16),
            pltpu.VMEM((2, N_DP, PIECE, HD), bf16),
            pltpu.VMEM((2, PROMPT, HD), bf16),
            pltpu.VMEM((64, 128), jnp.int32),
            pltpu.SMEM((64, 128), jnp.int32),
            dma((7,)), dma((RESP, 3)), dma((RESP, 14)), dma((RESP, 14)), dma((11,)), dma((11,)),
            dma((RESP, 2)), dma((RESP, 2)), dma((2,)), dma((2,)),
        ],
        compiler_params=pltpu.CompilerParams(
            collective_id=0, has_side_effects=True, vmem_limit_bytes=60 * 2**20
        ),
        cost_estimate=pl.CostEstimate(flops=19 * 10**9, bytes_accessed=20 * 10**6, transcendentals=6 * 10**6),
        name="attention_backward",
    )(group, length, owner, q, k, v, h, w, pk, pv)
    return pl.pallas_call(
        hand_over,
        out_shape=outs,
        in_specs=[any_] * 5,
        out_specs=(any_,) * 5,
        scratch_shapes=[pltpu.VMEM(a.shape, a.dtype) for a in outs] + [dma((8,)), dma((8,))],
        compiler_params=pltpu.CompilerParams(vmem_limit_bytes=60 * 2**20),
        name="hand_over",
    )(*grads)


def solution(mesh):
    whole = P("dp", "tensor")
    return jax.shard_map(
        body,
        mesh=mesh,
        in_specs=(whole, whole, whole, whole, P("tensor", None), whole, whole, P("dp"), P("dp"), P()),
        out_specs=(whole,) * 5,
        check_vma=False,
    )
```

```python
import functools

import jax
import jax.numpy as jnp
from jax import lax
from jax.experimental import pallas as pl
from jax.experimental.pallas import tpu as pltpu
from jax.sharding import PartitionSpec as P

HEADS_DEV = 8
HD = 128
PROMPT = 512
LEN = 256
KEYS = PROMPT + LEN
RESP = 4
N_DP = 16
SHARD = 640
PIECE = PROMPT // N_DP
EXTRA = 16
HPI = 4
HALVES = HEADS_DEV // HPI
HALF = LEN // 2
WIDE = HPI * LEN
SCALE = HD ** (-0.5)
SCALE_LOG2E = SCALE * 1.4426950408889634
f32, bf16 = jnp.float32, jnp.bfloat16
NT = (((1,), (1,)), ((), ()))
NN = (((1,), (0,)), ((), ()))

CUT_LO, CUT_P, CUT_HI = 80, 176, 192


def dotf(a, b, dims=NN):
    return lax.dot_general(a, b, dims, preferred_element_type=f32)


def kernel(
    group_ref, length_ref, owner_ref, q_in, k_in, v_in, h_in, w_in, pk_in, pv_in,
    dq_out, dk_out, dv_out, dpk_out, dpv_out,
    dh, w, q, g, dq, ko, vo, dko, dvo, tab, ka, va, kt, gacc, pb, prb, dsb, dka, dva, ctr, rbk, rbv, fin, frec, idx_v, idx_s,
    lsem, osem, d_send, d_recv, p_send, p_recv, a_send, a_recv, f_send, f_recv,
):
    dp = lax.axis_index("dp")
    ten = lax.axis_index("tensor")
    y, zl = lax.rem(ten, 4), ten // 4
    core, x, zh = lax.rem(dp, 2), lax.rem(dp // 2, 4), dp // 8

    def at_t(z_, y_):
        return z_ * 4 + lax.rem(y_ + 4, 4)

    def at_d(zh_, x_, c_):
        return zh_ * 8 + lax.rem(x_ + 4, 4) * 2 + c_

    t_plus, t_minus, t_z = at_t(zl, y + 1), at_t(zl, y - 1), at_t(1 - zl, y)
    d_plus, d_minus = at_d(zh, x + 1, core), at_d(zh, x - 1, core)
    d_zh, d_core = at_d(1 - zh, x, core), at_d(zh, x, 1 - core)
    place, place_zh = zh * 4 + x, (1 - zh) * 4 + x

    def cols(t_):
        return pl.ds(pl.multiple_of(t_ * SHARD, 128), SHARD)

    mine = [
        pltpu.make_async_copy(h_in, dh.at[:, cols(ten)], lsem.at[0]),
        pltpu.make_async_copy(pk_in, tab.at[0, place, core, 0:PROMPT], lsem.at[1]),
        pltpu.make_async_copy(pv_in, tab.at[1, place, core, 0:PROMPT], lsem.at[2]),
        pltpu.make_async_copy(q_in, q, lsem.at[3]),
        pltpu.make_async_copy(k_in, ko, lsem.at[4]),
        pltpu.make_async_copy(v_in, vo, lsem.at[5]),
        pltpu.make_async_copy(w_in, w, lsem.at[6]),
    ]
    for one in mine:
        one.start()

    slots = [owner_ref[group_ref[j]] for j in range(RESP)]
    row = lax.broadcasted_iota(jnp.int32, (EXTRA, HD), 0)
    filled = jnp.full((EXTRA, HD), -100, jnp.int32)
    for j in range(RESP):
        filled = jnp.where(row == j, slots[j], filled)
    for i in range(2):
        tab[i, place, core, PROMPT:] = filled.astype(f32).astype(bf16)

    barrier = pltpu.get_barrier_semaphore()
    for t_ in (t_plus, t_minus, t_z):
        pl.semaphore_signal(barrier, inc=1, device_id={"tensor": t_}, device_id_type=pl.DeviceIdType.MESH)
    for d_ in (d_plus, d_minus, d_zh, d_core):
        pl.semaphore_signal(barrier, inc=1, device_id={"dp": d_}, device_id_type=pl.DeviceIdType.MESH)
    for one in mine[:3]:
        one.wait()
    pl.semaphore_wait(barrier, 7)

    def send(src, dst, ss, rs, axis, target):
        pltpu.make_async_remote_copy(
            src_ref=src, dst_ref=dst, send_sem=ss, recv_sem=rs, device_id={axis: target},
            device_id_type=pl.DeviceIdType.MESH,
        ).start()

    def landed(ref, sem):
        pltpu.make_async_copy(ref, ref, sem).wait()

    def far(z_, y_):
        return at_t(z_, y_)

    nz = 1 - zl
    messages = [
        (ten, far(zl, y - 1), 0, HALF, t_plus),
        (ten, far(zl, y + 1), 0, HALF, t_minus),
        (ten, t_z, 0, HALF, t_z),
        (ten, far(zl, y - 1), HALF, LEN, t_plus),
        (ten, far(zl, y + 1), HALF, LEN, t_minus),
        (ten, t_z, HALF, LEN, t_z),
        (t_z, far(nz, y - 1), 0, CUT_P, t_plus),
        (t_z, far(nz, y + 1), 0, CUT_P, t_minus),
        (t_minus, far(zl, y + 2), CUT_LO, CUT_HI, t_plus),
        (t_plus, far(zl, y + 2), 0, CUT_LO, t_minus),
        (t_plus, far(zl, y + 2), CUT_HI, LEN, t_minus),
        (t_minus, far(nz, y - 1), CUT_P, LEN, t_z),
        (t_plus, far(nz, y + 1), CUT_P, LEN, t_z),
        (far(nz, y - 1), far(nz, y + 2), CUT_LO, CUT_P, t_plus),
        (far(nz, y + 1), far(nz, y + 2), 0, CUT_LO, t_minus),
        (far(zl, y + 2), far(nz, y + 2), CUT_P, CUT_HI, t_z),
        (far(zl, y + 2), far(nz, y + 2), CUT_HI, LEN, t_z),
    ]
    steps = ((0, 6), (6, 13), (13, 17))

    def part(c, shard, lo, hi):
        return dh.at[pl.ds(pl.multiple_of(c * LEN + lo, 16), hi - lo), cols(shard)]

    def h_send(c, step, some=None):
        for m in range(*(some or steps[step])):
            source, _, lo, hi, target = messages[m]
            block = part(c, source, lo, hi)
            send(block, block, d_send.at[c, m], d_recv.at[c, m], "tensor", target)

    def h_wait(c, step):
        for m in range(*steps[step]):
            _, got, lo, hi, _ = messages[m]
            landed(part(c, got, lo, hi), d_recv.at[c, m])

    def h_done(c):
        for m in range(len(messages)):
            source, _, lo, hi, _ = messages[m]
            landed(part(c, source, lo, hi), d_send.at[c, m])

    def pair(p_, c_):
        return tab.at[:, p_, c_]

    def spot(zh_, x_):
        return zh_ * 4 + lax.rem(x_ + 4, 4)

    nh = 1 - zh

    def line(zh_, c_):
        return tab.at[:, pl.ds(zh_ * 4, 4), c_]

    prompts = [
        (pair(place, core), pair(place_zh, core), d_zh),
        (pair(place, core), pair(spot(zh, x - 1), core), d_plus),
        (pair(place, core), pair(spot(zh, x + 1), core), d_minus),
        (pair(place_zh, core), pair(spot(nh, x - 1), core), d_plus),
        (pair(place_zh, core), pair(spot(nh, x + 1), core), d_minus),
        (tab.at[0, spot(zh, x - 1), core], tab.at[0, spot(zh, x + 2), core], d_plus),
        (tab.at[1, spot(zh, x + 1), core], tab.at[1, spot(zh, x + 2), core], d_minus),
        (tab.at[0, spot(nh, x - 1), core], tab.at[0, spot(nh, x + 2), core], d_plus),
        (tab.at[1, spot(nh, x + 1), core], tab.at[1, spot(nh, x + 2), core], d_minus),
        (line(zh, core), line(zh, 1 - core), d_core),
        (line(nh, core), line(nh, 1 - core), d_core),
    ]

    def p_go(*which):
        for m in which:
            block, _, target = prompts[m]
            send(block, block, p_send.at[m], p_recv.at[m], "dp", target)

    def p_wait(*which):
        for m in which:
            landed(prompts[m][1], p_recv.at[m])

    def spread(block, landing, ss, rs):
        for k in range(1, N_DP):
            peer = lax.rem(dp + k, N_DP)
            send(block(peer), landing, ss, rs, "dp", peer)
        pltpu.make_async_copy(block(dp), landing, rs).start()

    p_go(0, 1, 2)
    h_send(0, 0)
    h_send(1, 0)
    p_wait(1, 2)
    p_go(5, 6)
    h_wait(0, 0)
    h_send(0, 1)
    h_send(2, 0, (0, 3))
    p_wait(0)
    p_go(3, 4)

    h_wait(1, 0)
    p_wait(3, 4)
    p_go(7, 8)
    p_wait(5, 6)
    p_go(9)
    h_wait(0, 1)
    h_send(0, 2)
    h_send(1, 1)
    h_send(2, 0, (3, 6))
    h_send(3, 0, (0, 3))
    p_wait(7, 8)
    p_go(10)
    for one in mine[3:]:
        one.wait()
    p_wait(9, 10)


    by_row = tab[0, :, :, PROMPT:].astype(f32)[:, :, 0:8].reshape(128, 128)
    by_lane = by_row.T
    i_row = lax.broadcasted_iota(jnp.int32, (128, 128), 0)
    i_lane = lax.broadcasted_iota(jnp.int32, (128, 128), 1)
    before = jnp.where((by_row == by_lane) & (i_row < i_lane), 1.0, 0.0)
    rank = jnp.sum(before, 0, keepdims=True)
    rank = jnp.broadcast_to(4.0 * by_lane[0:1] + rank, (64, 128))
    number = (lax.shift_right_logical(i_lane, 3) * RESP + (i_lane & 7)).astype(f32)
    hit = jnp.where(rank == i_row[:64].astype(f32), number[:64], 0.0)
    index = jnp.sum(hit, 1, keepdims=True)
    idx_v[...] = jnp.broadcast_to(index, (64, 128)).astype(jnp.int32)
    to_s = pltpu.make_async_copy(idx_v, idx_s, lsem.at[0])
    to_s.start()

    key_at = lax.broadcasted_iota(jnp.int32, (LEN, WIDE), 0)
    row_at = lax.rem(lax.broadcasted_iota(jnp.int32, (LEN, WIDE), 1), LEN)
    causal = key_at <= row_at
    t_at = lax.broadcasted_iota(jnp.int32, (HEADS_DEV * HD, LEN), 1)

    def give(c, i):
        spread(lambda k: ctr.at[c, i, k], (rbk, rbv)[i].at[c, dp], a_send.at[c, i], a_recv.at[c, i])

    def add_up(i):
        for c in range(RESP):
            landed((rbk, rbv)[i].at[c], a_recv.at[c, i])

        @pl.loop(1, N_DP + 1)
        def _(n):
            s = lax.rem(dp + n, N_DP)
            total = jnp.zeros((PIECE, HD), f32)
            for k in range(RESP):
                r = idx_s[s * RESP + k, 0]
                total += (rbk, rbv)[i][r & (RESP - 1), lax.shift_right_logical(r, 2) & (N_DP - 1)].astype(f32)
            fin[i, s] = total.astype(bf16)
            landing = frec.at[i, pl.ds(dp * PIECE, PIECE)]

            @pl.when(n < N_DP)
            def _():
                send(fin.at[i, s], landing, f_send.at[i], f_recv.at[i], "dp", s)

            @pl.when(n == N_DP)
            def _():
                pltpu.make_async_copy(fin.at[i, s], landing, f_recv.at[i]).start()

    def rows_of(c):
        return pl.ds(pl.multiple_of(c * LEN, LEN), LEN)

    def heads(ref, c, h):
        return jnp.concatenate(
            [ref[rows_of(c), pl.ds(pl.multiple_of((h * HPI + i) * HD, HD), HD)] for i in range(HPI)], 0
        )

    def load_keys(c):
        slot = owner_ref[group_ref[c]]
        spot_slot = lax.shift_right_logical(slot, 1) & 7
        ka[0:PROMPT] = tab[0, spot_slot, slot & 1, 0:PROMPT]
        va[0:PROMPT] = tab[1, spot_slot, slot & 1, 0:PROMPT]
        ka[PROMPT:KEYS] = ko[rows_of(c)]
        va[PROMPT:KEYS] = vo[rows_of(c)]
        kt[...] = ka[...].astype(f32).T.astype(bf16)

    def probs(c, h):
        s = dotf(ka[...], heads(q, c, h), NT)
        so = jnp.where(causal, s[PROMPT:], -jnp.inf)
        sp = s[:PROMPT]
        m = jnp.maximum(jnp.max(sp, 0, keepdims=True), jnp.max(so, 0, keepdims=True))
        ep = jnp.exp2((sp - m) * SCALE_LOG2E)
        eo = jnp.exp2((so - m) * SCALE_LOG2E)
        inv = 1.0 / (jnp.sum(ep, 0, keepdims=True) + jnp.sum(eo, 0, keepdims=True))
        return jnp.concatenate([ep * inv, eo * inv], 0)

    def dscore(c, h, p, pr):
        d = dotf(va[...], heads(g, c, h), NT)
        delta = jnp.sum(pr.astype(f32) * d, 0, keepdims=True)
        return (p * (d - delta)).astype(bf16)

    def query_grad(c, h, ds):
        dqt = dotf(kt[...], ds) * SCALE
        for i in range(HPI):
            head = pl.ds(pl.multiple_of((h * HPI + i) * HD, HD), HD)
            dq[rows_of(c), head] = dqt[:, i * LEN : (i + 1) * LEN].T.astype(bf16)

    def shards(c, *which):
        return sum(dotf(w[:, cols(t_)], dh[rows_of(c), cols(t_)], NT) for t_ in which)

    def grad_rows(c, grad):
        g[rows_of(c), :] = jnp.where(t_at < length_ref[c], grad, 0.0).T.astype(bf16)

    def pieces(c, i, total):
        ctr[c, i] = total.astype(bf16).reshape(N_DP, PIECE, HD)
        give(c, i)

    def results(c):
        rows = rows_of(c)
        dko[rows] = (dka[PROMPT:KEYS] * SCALE).astype(bf16)
        dvo[rows] = dva[PROMPT:KEYS].astype(bf16)
        for n, (block, out) in enumerate(((dq, dq_out), (dko, dk_out), (dvo, dv_out))):
            pltpu.make_async_copy(block.at[rows], out.at[rows], osem.at[c, n]).start()

    final = RESP - 1
    load_keys(final)

    @pl.loop(0, HALVES)
    def _(h):
        p = probs(final, h)
        pb[h] = p
        prb[h] = p.astype(bf16)

    @pl.loop(0, final)
    def _(c):
        load_keys(c)
        dka[...] = jnp.zeros_like(dka)
        dva[...] = jnp.zeros_like(dva)
        h_wait(c, 2)
        grad_rows(c, dotf(w[...], dh[rows_of(c), :], NT))

        @pl.loop(0, HALVES)
        def _(h):
            p = probs(c, h)
            pr = p.astype(bf16)
            ds = dscore(c, h, p, pr)
            dva[...] += dotf(pr, heads(g, c, h))
            dka[...] += dotf(ds, heads(q, c, h))
            query_grad(c, h, ds)

            @pl.when(h == 0)
            def _():
                h_wait(c + 1, 1)
                h_send(c + 1, 2)

        @pl.when(c <= 1)
        def _():
            h_wait(c + 2, 0)
            h_send(c + 2, 1)

        @pl.when(c == 0)
        def _():
            h_send(final, 0, (3, 6))

        pieces(c, 1, dva[0:PROMPT])
        pieces(c, 0, dka[0:PROMPT] * SCALE)
        results(c)

        @pl.when(c == 1)
        def _():
            gacc[...] = shards(final, ten, t_plus, t_minus, t_z)

    gacc[...] += shards(final, far(zl, y + 2), far(nz, y - 1), far(nz, y + 1))
    load_keys(final)
    dka[...] = jnp.zeros_like(dka)
    dva[...] = jnp.zeros_like(dva)
    h_wait(final, 2)
    grad_rows(final, gacc[...] + shards(final, far(nz, y + 2)))

    @pl.loop(0, HALVES)
    def _(h):
        dva[...] += dotf(prb[h], heads(g, final, h))

    pieces(final, 1, dva[0:PROMPT])

    @pl.loop(0, HALVES)
    def _(h):
        ds = dscore(final, h, pb[h], prb[h])
        dsb[h] = ds
        dka[...] += dotf(ds, heads(q, final, h))

    pieces(final, 0, dka[0:PROMPT] * SCALE)
    to_s.wait()
    add_up(1)

    @pl.loop(0, HALVES)
    def _(h):
        query_grad(final, h, dsb[h])

    results(final)
    add_up(0)
    for c in range(RESP):
        h_done(c)
        for i in range(2):
            landed(ctr.at[c, i, 0:15], a_send.at[c, i])
        done = pl.ds(c * LEN, LEN)
        for n, (block, out) in enumerate(((dq, dq_out), (dko, dk_out), (dvo, dv_out))):
            pltpu.make_async_copy(block.at[done], out.at[done], osem.at[c, n]).wait()
    for m, (block, _, _) in enumerate(prompts):
        landed(block, p_send.at[m])
    last = [
        pltpu.make_async_copy(frec.at[1], dpv_out, lsem.at[1]),
        pltpu.make_async_copy(frec.at[0], dpk_out, lsem.at[2]),
    ]
    for i in (1, 0):
        landed(frec.at[i], f_recv.at[i])
        last[1 - i].start()
    for i in (1, 0):
        landed(fin.at[i, 0:15], f_send.at[i])
        last[1 - i].wait()


def hand_over(*refs):
    n = (len(refs) - 2) // 3
    sources, targets, held, sem_in, sem_out = refs[:n], refs[n : 2 * n], refs[2 * n : 3 * n], refs[-2], refs[-1]
    parts = [(i, pl.ds(k * LEN, LEN)) for i in range(n) for k in range(sources[i].shape[0] // LEN if i == 0 else 1)]
    parts = [(i, p if i == 0 else pl.ds(0, sources[i].shape[0])) for i, p in parts]
    into = [
        pltpu.make_async_copy(sources[i].at[p], held[i].at[p], sem_in.at[k]) for k, (i, p) in enumerate(parts)
    ]
    out = [
        pltpu.make_async_copy(held[i].at[p], targets[i].at[p], sem_out.at[k]) for k, (i, p) in enumerate(parts)
    ]
    for one in into:
        one.start()
    for first, second in zip(into, out):
        first.wait()
        second.start()
    for one in out:
        one.wait()


def body(q, k, v, h, w, pk, pv, group, length, owner):
    def out(a):
        return jax.ShapeDtypeStruct(a.shape, a.dtype)

    any_, smem = (pl.BlockSpec(memory_space=m) for m in (pl.ANY, pltpu.SMEM))
    dma = pltpu.SemaphoreType.DMA
    outs = (out(q), out(k), out(v), out(pk), out(pv))
    grads = pl.pallas_call(
        kernel,
        out_shape=outs,
        in_specs=[smem] * 3 + [any_] * 7,
        out_specs=(any_,) * 5,
        scratch_shapes=[
            pltpu.VMEM((RESP * LEN, 8 * SHARD), bf16),
            pltpu.VMEM((HEADS_DEV * HD, 8 * SHARD), bf16),
            pltpu.VMEM((RESP * LEN, HEADS_DEV * HD), bf16),
            pltpu.VMEM((RESP * LEN, HEADS_DEV * HD), bf16),
            pltpu.VMEM((RESP * LEN, HEADS_DEV * HD), bf16),
            pltpu.VMEM((RESP * LEN, HD), bf16),
            pltpu.VMEM((RESP * LEN, HD), bf16),
            pltpu.VMEM((RESP * LEN, HD), bf16),
            pltpu.VMEM((RESP * LEN, HD), bf16),
            pltpu.VMEM((2, 8, 2, PROMPT + EXTRA, HD), bf16),
            pltpu.VMEM((KEYS, HD), bf16),
            pltpu.VMEM((KEYS, HD), bf16),
            pltpu.VMEM((HD, KEYS), bf16),
            pltpu.VMEM((HEADS_DEV * HD, LEN), f32),
            pltpu.VMEM((HALVES, KEYS, WIDE), f32),
            pltpu.VMEM((HALVES, KEYS, WIDE), bf16),
            pltpu.VMEM((HALVES, KEYS, WIDE), bf16),
            pltpu.VMEM((KEYS, HD), f32),
            pltpu.VMEM((KEYS, HD), f32),
            pltpu.VMEM((RESP, 2, N_DP, PIECE, HD), bf16),
            pltpu.VMEM((RESP, N_DP, PIECE, HD), bf16),
            pltpu.VMEM((RESP, N_DP, PIECE, HD), bf16),
            pltpu.VMEM((2, N_DP, PIECE, HD), bf16),
            pltpu.VMEM((2, PROMPT, HD), bf16),
            pltpu.VMEM((64, 128), jnp.int32),
            pltpu.SMEM((64, 128), jnp.int32),
            dma((7,)), dma((RESP, 3)), dma((RESP, 17)), dma((RESP, 17)), dma((11,)), dma((11,)),
            dma((RESP, 2)), dma((RESP, 2)), dma((2,)), dma((2,)),
        ],
        compiler_params=pltpu.CompilerParams(
            collective_id=0, has_side_effects=True, vmem_limit_bytes=60 * 2**20
        ),
        cost_estimate=pl.CostEstimate(flops=19 * 10**9, bytes_accessed=20 * 10**6, transcendentals=6 * 10**6),
        name="attention_backward",
    )(group, length, owner, q, k, v, h, w, pk, pv)
    return pl.pallas_call(
        hand_over,
        out_shape=outs,
        in_specs=[any_] * 5,
        out_specs=(any_,) * 5,
        scratch_shapes=[pltpu.VMEM(a.shape, a.dtype) for a in outs] + [dma((8,)), dma((8,))],
        compiler_params=pltpu.CompilerParams(vmem_limit_bytes=60 * 2**20),
        name="hand_over",
    )(*grads)


def solution(mesh):
    whole = P("dp", "tensor")
    return jax.shard_map(
        body,
        mesh=mesh,
        in_specs=(whole, whole, whole, whole, P("tensor", None), whole, whole, P("dp"), P("dp"), P()),
        out_specs=(whole,) * 5,
        check_vma=False,
    )
```

```python
import functools

import jax
import jax.numpy as jnp
from jax import lax
from jax.experimental import pallas as pl
from jax.experimental.pallas import tpu as pltpu
from jax.sharding import PartitionSpec as P

HEADS_DEV = 8
HD = 128
PROMPT = 512
LEN = 256
KEYS = PROMPT + LEN
RESP = 4
N_DP = 16
SHARD = 640
PIECE = PROMPT // N_DP
EXTRA = 16
HPI = 4
HALVES = HEADS_DEV // HPI
HALF = LEN // 2
WIDE = HPI * LEN
SCALE = HD ** (-0.5)
SCALE_LOG2E = SCALE * 1.4426950408889634
f32, bf16 = jnp.float32, jnp.bfloat16
NT = (((1,), (1,)), ((), ()))
NN = (((1,), (0,)), ((), ()))

CUT_LO, CUT_P, CUT_HI = 80, 160, 208


def dotf(a, b, dims=NN):
    return lax.dot_general(a, b, dims, preferred_element_type=f32)


def kernel(
    group_ref, length_ref, owner_ref, q_in, k_in, v_in, h_in, w_in, pk_in, pv_in,
    dq, dko, dvo, dpk, dpv,
    dh, w, q, g, ko, vo, tab, ka, va, kt, gacc, pb, prb, dsb, dka, dva, ctr, rbk, rbv, fin, frec, idx_v, idx_s,
    lsem, d_send, d_recv, p_send, p_recv, a_send, a_recv, f_send, f_recv,
):
    dp = lax.axis_index("dp")
    ten = lax.axis_index("tensor")
    y, zl = lax.rem(ten, 4), ten // 4
    core, x, zh = lax.rem(dp, 2), lax.rem(dp // 2, 4), dp // 8

    def at_t(z_, y_):
        return z_ * 4 + lax.rem(y_ + 4, 4)

    def at_d(zh_, x_, c_):
        return zh_ * 8 + lax.rem(x_ + 4, 4) * 2 + c_

    t_plus, t_minus, t_z = at_t(zl, y + 1), at_t(zl, y - 1), at_t(1 - zl, y)
    d_plus, d_minus = at_d(zh, x + 1, core), at_d(zh, x - 1, core)
    d_zh, d_core = at_d(1 - zh, x, core), at_d(zh, x, 1 - core)
    place, place_zh = zh * 4 + x, (1 - zh) * 4 + x

    def cols(t_):
        return pl.ds(pl.multiple_of(t_ * SHARD, 128), SHARD)

    mine = [
        pltpu.make_async_copy(h_in, dh.at[:, cols(ten)], lsem.at[0]),
        pltpu.make_async_copy(pk_in, tab.at[0, place, core, 0:PROMPT], lsem.at[1]),
        pltpu.make_async_copy(pv_in, tab.at[1, place, core, 0:PROMPT], lsem.at[2]),
        pltpu.make_async_copy(q_in, q, lsem.at[3]),
        pltpu.make_async_copy(k_in, ko, lsem.at[4]),
        pltpu.make_async_copy(v_in, vo, lsem.at[5]),
        pltpu.make_async_copy(w_in, w, lsem.at[6]),
    ]
    for one in mine:
        one.start()

    slots = [owner_ref[group_ref[j]] for j in range(RESP)]
    row = lax.broadcasted_iota(jnp.int32, (EXTRA, HD), 0)
    filled = jnp.full((EXTRA, HD), -100, jnp.int32)
    for j in range(RESP):
        filled = jnp.where(row == j, slots[j], filled)
    for i in range(2):
        tab[i, place, core, PROMPT:] = filled.astype(f32).astype(bf16)

    barrier = pltpu.get_barrier_semaphore()
    for t_ in (t_plus, t_minus, t_z):
        pl.semaphore_signal(barrier, inc=1, device_id={"tensor": t_}, device_id_type=pl.DeviceIdType.MESH)
    for d_ in (d_plus, d_minus, d_zh, d_core):
        pl.semaphore_signal(barrier, inc=1, device_id={"dp": d_}, device_id_type=pl.DeviceIdType.MESH)
    for one in mine[:3]:
        one.wait()
    pl.semaphore_wait(barrier, 7)

    def send(src, dst, ss, rs, axis, target):
        pltpu.make_async_remote_copy(
            src_ref=src, dst_ref=dst, send_sem=ss, recv_sem=rs, device_id={axis: target},
            device_id_type=pl.DeviceIdType.MESH,
        ).start()

    def landed(ref, sem):
        pltpu.make_async_copy(ref, ref, sem).wait()

    def far(z_, y_):
        return at_t(z_, y_)

    nz = 1 - zl
    messages = [
        (ten, far(zl, y - 1), 0, HALF, t_plus),
        (ten, far(zl, y + 1), 0, HALF, t_minus),
        (ten, t_z, 0, HALF, t_z),
        (ten, far(zl, y - 1), HALF, LEN, t_plus),
        (ten, far(zl, y + 1), HALF, LEN, t_minus),
        (ten, t_z, HALF, LEN, t_z),
        (t_z, far(nz, y - 1), 0, CUT_P, t_plus),
        (t_z, far(nz, y + 1), 0, CUT_P, t_minus),
        (t_minus, far(zl, y + 2), CUT_LO, CUT_HI, t_plus),
        (t_plus, far(zl, y + 2), 0, CUT_LO, t_minus),
        (t_plus, far(zl, y + 2), CUT_HI, LEN, t_minus),
        (t_minus, far(nz, y - 1), CUT_P, LEN, t_z),
        (t_plus, far(nz, y + 1), CUT_P, LEN, t_z),
        (far(nz, y - 1), far(nz, y + 2), CUT_LO, CUT_P, t_plus),
        (far(nz, y + 1), far(nz, y + 2), 0, CUT_LO, t_minus),
        (far(zl, y + 2), far(nz, y + 2), CUT_P, CUT_HI, t_z),
        (far(zl, y + 2), far(nz, y + 2), CUT_HI, LEN, t_z),
    ]
    steps = ((0, 6), (6, 13), (13, 17))

    def part(c, shard, lo, hi):
        return dh.at[pl.ds(pl.multiple_of(c * LEN + lo, 16), hi - lo), cols(shard)]

    def h_send(c, step, some=None):
        for m in range(*(some or steps[step])):
            source, _, lo, hi, target = messages[m]
            block = part(c, source, lo, hi)
            send(block, block, d_send.at[c, m], d_recv.at[c, m], "tensor", target)

    def h_wait(c, step):
        for m in range(*steps[step]):
            _, got, lo, hi, _ = messages[m]
            landed(part(c, got, lo, hi), d_recv.at[c, m])

    def h_done(c):
        for m in range(len(messages)):
            source, _, lo, hi, _ = messages[m]
            landed(part(c, source, lo, hi), d_send.at[c, m])

    def pair(p_, c_):
        return tab.at[:, p_, c_]

    def spot(zh_, x_):
        return zh_ * 4 + lax.rem(x_ + 4, 4)

    nh = 1 - zh

    def line(zh_, c_):
        return tab.at[:, pl.ds(zh_ * 4, 4), c_]

    prompts = [
        (pair(place, core), pair(place_zh, core), d_zh),
        (pair(place, core), pair(spot(zh, x - 1), core), d_plus),
        (pair(place, core), pair(spot(zh, x + 1), core), d_minus),
        (pair(place_zh, core), pair(spot(nh, x - 1), core), d_plus),
        (pair(place_zh, core), pair(spot(nh, x + 1), core), d_minus),
        (tab.at[0, spot(zh, x - 1), core], tab.at[0, spot(zh, x + 2), core], d_plus),
        (tab.at[1, spot(zh, x + 1), core], tab.at[1, spot(zh, x + 2), core], d_minus),
        (tab.at[0, spot(nh, x - 1), core], tab.at[0, spot(nh, x + 2), core], d_plus),
        (tab.at[1, spot(nh, x + 1), core], tab.at[1, spot(nh, x + 2), core], d_minus),
        (line(zh, core), line(zh, 1 - core), d_core),
        (line(nh, core), line(nh, 1 - core), d_core),
    ]

    def p_go(*which):
        for m in which:
            block, _, target = prompts[m]
            send(block, block, p_send.at[m], p_recv.at[m], "dp", target)

    def p_wait(*which):
        for m in which:
            landed(prompts[m][1], p_recv.at[m])

    def spread(block, landing, ss, rs):
        for k in range(1, N_DP):
            peer = lax.rem(dp + k, N_DP)
            send(block(peer), landing, ss, rs, "dp", peer)
        pltpu.make_async_copy(block(dp), landing, rs).start()

    h_send(0, 0)
    p_go(0, 1, 2)
    h_send(1, 0)
    p_wait(1, 2)
    p_go(5, 6)
    p_wait(0)
    p_go(3, 4)
    h_wait(0, 0)
    h_send(0, 1)
    h_send(2, 0, (0, 3))
    h_wait(1, 0)
    p_wait(3, 4)
    p_go(7, 8)
    p_wait(5, 6)
    p_go(9)
    h_wait(0, 1)
    h_send(0, 2)
    h_send(1, 1)
    h_send(2, 0, (3, 6))
    h_send(3, 0, (0, 3))
    p_wait(7, 8)
    p_go(10)
    for one in mine[3:]:
        one.wait()
    p_wait(9, 10)


    by_row = tab[0, :, :, PROMPT:].astype(f32)[:, :, 0:8].reshape(128, 128)
    by_lane = by_row.T
    i_row = lax.broadcasted_iota(jnp.int32, (128, 128), 0)
    i_lane = lax.broadcasted_iota(jnp.int32, (128, 128), 1)
    before = jnp.where((by_row == by_lane) & (i_row < i_lane), 1.0, 0.0)
    rank = jnp.sum(before, 0, keepdims=True)
    rank = jnp.broadcast_to(4.0 * by_lane[0:1] + rank, (64, 128))
    number = (lax.shift_right_logical(i_lane, 3) * RESP + (i_lane & 7)).astype(f32)
    hit = jnp.where(rank == i_row[:64].astype(f32), number[:64], 0.0)
    index = jnp.sum(hit, 1, keepdims=True)
    idx_v[...] = jnp.broadcast_to(index, (64, 128)).astype(jnp.int32)
    to_s = pltpu.make_async_copy(idx_v, idx_s, lsem.at[0])
    to_s.start()

    key_at = lax.broadcasted_iota(jnp.int32, (LEN, WIDE), 0)
    row_at = lax.rem(lax.broadcasted_iota(jnp.int32, (LEN, WIDE), 1), LEN)
    causal = key_at <= row_at
    t_at = lax.broadcasted_iota(jnp.int32, (HEADS_DEV * HD, LEN), 1)

    def give(c, i):
        spread(lambda k: ctr.at[c, i, k], (rbk, rbv)[i].at[c, dp], a_send.at[c, i], a_recv.at[c, i])

    def add_up(i):
        for c in range(RESP):
            landed((rbk, rbv)[i].at[c], a_recv.at[c, i])

        @pl.loop(1, N_DP + 1)
        def _(n):
            s = lax.rem(dp + n, N_DP)
            total = jnp.zeros((PIECE, HD), f32)
            for k in range(RESP):
                r = idx_s[s * RESP + k, 0]
                total += (rbk, rbv)[i][r & (RESP - 1), lax.shift_right_logical(r, 2) & (N_DP - 1)].astype(f32)
            fin[i, s] = total.astype(bf16)
            landing = frec.at[i, pl.ds(dp * PIECE, PIECE)]

            @pl.when(n < N_DP)
            def _():
                send(fin.at[i, s], landing, f_send.at[i], f_recv.at[i], "dp", s)

            @pl.when(n == N_DP)
            def _():
                pltpu.make_async_copy(fin.at[i, s], landing, f_recv.at[i]).start()

    def rows_of(c):
        return pl.ds(pl.multiple_of(c * LEN, LEN), LEN)

    def heads(ref, c, h):
        return jnp.concatenate(
            [ref[rows_of(c), pl.ds(pl.multiple_of((h * HPI + i) * HD, HD), HD)] for i in range(HPI)], 0
        )

    def load_keys(c):
        slot = owner_ref[group_ref[c]]
        spot_slot = lax.shift_right_logical(slot, 1) & 7
        ka[0:PROMPT] = tab[0, spot_slot, slot & 1, 0:PROMPT]
        va[0:PROMPT] = tab[1, spot_slot, slot & 1, 0:PROMPT]
        ka[PROMPT:KEYS] = ko[rows_of(c)]
        va[PROMPT:KEYS] = vo[rows_of(c)]
        kt[...] = ka[...].astype(f32).T.astype(bf16)

    def probs(c, h):
        s = dotf(ka[...], heads(q, c, h), NT)
        so = jnp.where(causal, s[PROMPT:], -jnp.inf)
        sp = s[:PROMPT]
        m = jnp.maximum(jnp.max(sp, 0, keepdims=True), jnp.max(so, 0, keepdims=True))
        ep = jnp.exp2((sp - m) * SCALE_LOG2E)
        eo = jnp.exp2((so - m) * SCALE_LOG2E)
        inv = 1.0 / (jnp.sum(ep, 0, keepdims=True) + jnp.sum(eo, 0, keepdims=True))
        return jnp.concatenate([ep * inv, eo * inv], 0)

    def dscore(c, h, p, pr):
        d = dotf(va[...], heads(g, c, h), NT)
        delta = jnp.sum(pr.astype(f32) * d, 0, keepdims=True)
        return (p * (d - delta)).astype(bf16)

    def query_grad(c, h, ds):
        dqt = dotf(kt[...], ds) * SCALE
        for i in range(HPI):
            head = pl.ds(pl.multiple_of((h * HPI + i) * HD, HD), HD)
            dq[rows_of(c), head] = dqt[:, i * LEN : (i + 1) * LEN].T.astype(bf16)

    def shards(c, *which):
        return sum(dotf(w[:, cols(t_)], dh[rows_of(c), cols(t_)], NT) for t_ in which)

    def grad_rows(c, grad):
        g[rows_of(c), :] = jnp.where(t_at < length_ref[c], grad, 0.0).T.astype(bf16)

    def pieces(c, i, total):
        ctr[c, i] = total.astype(bf16).reshape(N_DP, PIECE, HD)
        give(c, i)

    def results(c):
        rows = rows_of(c)
        dko[rows] = (dka[PROMPT:KEYS] * SCALE).astype(bf16)
        dvo[rows] = dva[PROMPT:KEYS].astype(bf16)

    final = RESP - 1
    @pl.loop(0, final)
    def _(c):
        load_keys(c)
        dka[...] = jnp.zeros_like(dka)
        dva[...] = jnp.zeros_like(dva)
        h_wait(c, 2)
        grad_rows(c, dotf(w[...], dh[rows_of(c), :], NT))

        @pl.loop(0, HALVES)
        def _(h):
            p = probs(c, h)
            pr = p.astype(bf16)
            ds = dscore(c, h, p, pr)
            dva[...] += dotf(pr, heads(g, c, h))
            dka[...] += dotf(ds, heads(q, c, h))
            query_grad(c, h, ds)

            @pl.when(h == 0)
            def _():
                h_wait(c + 1, 1)
                h_send(c + 1, 2)

        @pl.when(c <= 1)
        def _():
            h_wait(c + 2, 0)
            h_send(c + 2, 1)

        @pl.when(c == 0)
        def _():
            h_send(final, 0, (3, 6))

        pieces(c, 1, dva[0:PROMPT])
        pieces(c, 0, dka[0:PROMPT] * SCALE)
        results(c)

        @pl.when(c == 0)
        def _():
            load_keys(final)

            @pl.loop(0, HALVES)
            def _(h):
                p = probs(final, h)
                pb[h] = p
                prb[h] = p.astype(bf16)

        @pl.when(c == 1)
        def _():
            gacc[...] = shards(final, ten, t_plus, t_minus, t_z)

    gacc[...] += shards(final, far(zl, y + 2), far(nz, y - 1), far(nz, y + 1))
    load_keys(final)
    dka[...] = jnp.zeros_like(dka)
    dva[...] = jnp.zeros_like(dva)
    h_wait(final, 2)
    grad_rows(final, gacc[...] + shards(final, far(nz, y + 2)))

    @pl.loop(0, HALVES)
    def _(h):
        dva[...] += dotf(prb[h], heads(g, final, h))

    pieces(final, 1, dva[0:PROMPT])

    @pl.loop(0, HALVES)
    def _(h):
        ds = dscore(final, h, pb[h], prb[h])
        dsb[h] = ds
        dka[...] += dotf(ds, heads(q, final, h))

    pieces(final, 0, dka[0:PROMPT] * SCALE)
    to_s.wait()
    add_up(1)

    @pl.loop(0, HALVES)
    def _(h):
        query_grad(final, h, dsb[h])

    results(final)
    add_up(0)
    for c in range(RESP):
        h_done(c)
        for i in range(2):
            landed(ctr.at[c, i, 0:15], a_send.at[c, i])
    for m, (block, _, _) in enumerate(prompts):
        landed(block, p_send.at[m])
    for i, out in ((1, dpv), (0, dpk)):
        landed(frec.at[i], f_recv.at[i])
        out[...] = frec[i]
    for i in range(2):
        landed(fin.at[i, 0:15], f_send.at[i])


def hand_over(*refs):
    n = len(refs) // 2
    copies = [pltpu.make_async_copy(refs[i], refs[n + i], refs[-1].at[i]) for i in range(n)]
    for one in copies:
        one.start()
    for one in copies:
        one.wait()


def body(q, k, v, h, w, pk, pv, group, length, owner):
    def out(a):
        return jax.ShapeDtypeStruct(a.shape, a.dtype)

    any_, vmem, smem = (pl.BlockSpec(memory_space=m) for m in (pl.ANY, pltpu.VMEM, pltpu.SMEM))
    dma = pltpu.SemaphoreType.DMA
    outs = (out(q), out(k), out(v), out(pk), out(pv))
    grads = pl.pallas_call(
        kernel,
        out_shape=tuple(pltpu.VMEM(a.shape, a.dtype) for a in outs),
        in_specs=[smem] * 3 + [any_] * 7,
        out_specs=(vmem,) * 5,
        scratch_shapes=[
            pltpu.VMEM((RESP * LEN, 8 * SHARD), bf16),
            pltpu.VMEM((HEADS_DEV * HD, 8 * SHARD), bf16),
            pltpu.VMEM((RESP * LEN, HEADS_DEV * HD), bf16),
            pltpu.VMEM((RESP * LEN, HEADS_DEV * HD), bf16),
            pltpu.VMEM((RESP * LEN, HD), bf16),
            pltpu.VMEM((RESP * LEN, HD), bf16),
            pltpu.VMEM((2, 8, 2, PROMPT + EXTRA, HD), bf16),
            pltpu.VMEM((KEYS, HD), bf16),
            pltpu.VMEM((KEYS, HD), bf16),
            pltpu.VMEM((HD, KEYS), bf16),
            pltpu.VMEM((HEADS_DEV * HD, LEN), f32),
            pltpu.VMEM((HALVES, KEYS, WIDE), f32),
            pltpu.VMEM((HALVES, KEYS, WIDE), bf16),
            pltpu.VMEM((HALVES, KEYS, WIDE), bf16),
            pltpu.VMEM((KEYS, HD), f32),
            pltpu.VMEM((KEYS, HD), f32),
            pltpu.VMEM((RESP, 2, N_DP, PIECE, HD), bf16),
            pltpu.VMEM((RESP, N_DP, PIECE, HD), bf16),
            pltpu.VMEM((RESP, N_DP, PIECE, HD), bf16),
            pltpu.VMEM((2, N_DP, PIECE, HD), bf16),
            pltpu.VMEM((2, PROMPT, HD), bf16),
            pltpu.VMEM((64, 128), jnp.int32),
            pltpu.SMEM((64, 128), jnp.int32),
            dma((7,)), dma((RESP, 17)), dma((RESP, 17)), dma((11,)), dma((11,)),
            dma((RESP, 2)), dma((RESP, 2)), dma((2,)), dma((2,)),
        ],
        compiler_params=pltpu.CompilerParams(
            collective_id=0, has_side_effects=True, vmem_limit_bytes=56 * 2**20
        ),
        cost_estimate=pl.CostEstimate(flops=19 * 10**9, bytes_accessed=20 * 10**6, transcendentals=6 * 10**6),
        name="attention_backward",
    )(group, length, owner, q, k, v, h, w, pk, pv)
    return pl.pallas_call(
        hand_over,
        out_shape=outs,
        in_specs=[vmem] * 5,
        out_specs=(any_,) * 5,
        scratch_shapes=[dma((5,))],
        compiler_params=pltpu.CompilerParams(vmem_limit_bytes=4 * 2**20),
        name="hand_over",
    )(*(pltpu.with_memory_space_constraint(a, pltpu.VMEM) for a in grads))


def solution(mesh):
    whole = P("dp", "tensor")
    return jax.shard_map(
        body,
        mesh=mesh,
        in_specs=(whole, whole, whole, whole, P("tensor", None), whole, whole, P("dp"), P("dp"), P()),
        out_specs=(whole,) * 5,
        check_vma=False,
    )
```

```python
import functools

import jax
import jax.numpy as jnp
from jax import lax
from jax.experimental import pallas as pl
from jax.experimental.pallas import tpu as pltpu
from jax.sharding import PartitionSpec as P

HEADS_DEV = 8
HD = 128
PROMPT = 512
LEN = 256
KEYS = PROMPT + LEN
RESP = 4
N_DP = 16
SHARD = 640
PIECE = PROMPT // N_DP
EXTRA = 16
HPI = 4
HALVES = HEADS_DEV // HPI
HALF = LEN // 2
WIDE = HPI * LEN
SCALE = HD ** (-0.5)
SCALE_LOG2E = SCALE * 1.4426950408889634
f32, bf16 = jnp.float32, jnp.bfloat16
NT = (((1,), (1,)), ((), ()))
NN = (((1,), (0,)), ((), ()))

CUT_LO, CUT_P, CUT_HI = 80, 160, 208


def dotf(a, b, dims=NN):
    return lax.dot_general(a, b, dims, preferred_element_type=f32)


def kernel(
    group_ref, length_ref, owner_ref, q_in, k_in, v_in, h_in, w_in, pk_in, pv_in,
    dq, dko, dvo, dpk, dpv,
    dh, w, q, g, ko, vo, tab, ka, va, kt, gacc, pb, prb, dsb, dka, dva, ctr, rbk, rbv, fin, idx_v, idx_s,
    lsem, d_send, d_recv, p_send, p_recv, a_send, a_recv, f_send, f_recv,
):
    dp = lax.axis_index("dp")
    ten = lax.axis_index("tensor")
    y, zl = lax.rem(ten, 4), ten // 4
    core, x, zh = lax.rem(dp, 2), lax.rem(dp // 2, 4), dp // 8

    def at_t(z_, y_):
        return z_ * 4 + lax.rem(y_ + 4, 4)

    def at_d(zh_, x_, c_):
        return zh_ * 8 + lax.rem(x_ + 4, 4) * 2 + c_

    t_plus, t_minus, t_z = at_t(zl, y + 1), at_t(zl, y - 1), at_t(1 - zl, y)
    d_plus, d_minus = at_d(zh, x + 1, core), at_d(zh, x - 1, core)
    d_zh, d_core = at_d(1 - zh, x, core), at_d(zh, x, 1 - core)
    place, place_zh = zh * 4 + x, (1 - zh) * 4 + x

    def cols(t_):
        return pl.ds(pl.multiple_of(t_ * SHARD, 128), SHARD)

    mine = [
        pltpu.make_async_copy(h_in, dh.at[:, cols(ten)], lsem.at[0]),
        pltpu.make_async_copy(pk_in, tab.at[0, place, core, 0:PROMPT], lsem.at[1]),
        pltpu.make_async_copy(pv_in, tab.at[1, place, core, 0:PROMPT], lsem.at[2]),
        pltpu.make_async_copy(q_in, q, lsem.at[3]),
        pltpu.make_async_copy(k_in, ko, lsem.at[4]),
        pltpu.make_async_copy(v_in, vo, lsem.at[5]),
        pltpu.make_async_copy(w_in, w, lsem.at[6]),
    ]
    for one in mine:
        one.start()

    slots = [owner_ref[group_ref[j]] for j in range(RESP)]
    row = lax.broadcasted_iota(jnp.int32, (EXTRA, HD), 0)
    filled = jnp.full((EXTRA, HD), -100, jnp.int32)
    for j in range(RESP):
        filled = jnp.where(row == j, slots[j], filled)
    for i in range(2):
        tab[i, place, core, PROMPT:] = filled.astype(f32).astype(bf16)

    barrier = pltpu.get_barrier_semaphore()
    for t_ in (t_plus, t_minus, t_z):
        pl.semaphore_signal(barrier, inc=1, device_id={"tensor": t_}, device_id_type=pl.DeviceIdType.MESH)
    for d_ in (d_plus, d_minus, d_zh, d_core):
        pl.semaphore_signal(barrier, inc=1, device_id={"dp": d_}, device_id_type=pl.DeviceIdType.MESH)
    for one in mine[:3]:
        one.wait()
    pl.semaphore_wait(barrier, 7)

    def send(src, dst, ss, rs, axis, target):
        pltpu.make_async_remote_copy(
            src_ref=src, dst_ref=dst, send_sem=ss, recv_sem=rs, device_id={axis: target},
            device_id_type=pl.DeviceIdType.MESH,
        ).start()

    def landed(ref, sem):
        pltpu.make_async_copy(ref, ref, sem).wait()

    def far(z_, y_):
        return at_t(z_, y_)

    nz = 1 - zl
    messages = [
        (ten, far(zl, y - 1), 0, HALF, t_plus),
        (ten, far(zl, y + 1), 0, HALF, t_minus),
        (ten, t_z, 0, HALF, t_z),
        (ten, far(zl, y - 1), HALF, LEN, t_plus),
        (ten, far(zl, y + 1), HALF, LEN, t_minus),
        (ten, t_z, HALF, LEN, t_z),
        (t_z, far(nz, y - 1), 0, CUT_P, t_plus),
        (t_z, far(nz, y + 1), 0, CUT_P, t_minus),
        (t_minus, far(zl, y + 2), CUT_LO, CUT_HI, t_plus),
        (t_plus, far(zl, y + 2), 0, CUT_LO, t_minus),
        (t_plus, far(zl, y + 2), CUT_HI, LEN, t_minus),
        (t_minus, far(nz, y - 1), CUT_P, LEN, t_z),
        (t_plus, far(nz, y + 1), CUT_P, LEN, t_z),
        (far(nz, y - 1), far(nz, y + 2), CUT_LO, CUT_P, t_plus),
        (far(nz, y + 1), far(nz, y + 2), 0, CUT_LO, t_minus),
        (far(zl, y + 2), far(nz, y + 2), CUT_P, CUT_HI, t_z),
        (far(zl, y + 2), far(nz, y + 2), CUT_HI, LEN, t_z),
    ]
    steps = ((0, 6), (6, 13), (13, 17))

    def part(c, shard, lo, hi):
        return dh.at[pl.ds(pl.multiple_of(c * LEN + lo, 16), hi - lo), cols(shard)]

    def h_send(c, step, some=None):
        for m in range(*(some or steps[step])):
            source, _, lo, hi, target = messages[m]
            block = part(c, source, lo, hi)
            send(block, block, d_send.at[c, m], d_recv.at[c, m], "tensor", target)

    def h_wait(c, step):
        for m in range(*steps[step]):
            _, got, lo, hi, _ = messages[m]
            landed(part(c, got, lo, hi), d_recv.at[c, m])

    def h_done(c):
        for m in range(len(messages)):
            source, _, lo, hi, _ = messages[m]
            landed(part(c, source, lo, hi), d_send.at[c, m])

    def pair(p_, c_):
        return tab.at[:, p_, c_]

    def spot(zh_, x_):
        return zh_ * 4 + lax.rem(x_ + 4, 4)

    nh = 1 - zh

    def line(zh_, c_):
        return tab.at[:, pl.ds(zh_ * 4, 4), c_]

    prompts = [
        (pair(place, core), pair(place_zh, core), d_zh),
        (pair(place, core), pair(spot(zh, x - 1), core), d_plus),
        (pair(place, core), pair(spot(zh, x + 1), core), d_minus),
        (pair(place_zh, core), pair(spot(nh, x - 1), core), d_plus),
        (pair(place_zh, core), pair(spot(nh, x + 1), core), d_minus),
        (tab.at[0, spot(zh, x - 1), core], tab.at[0, spot(zh, x + 2), core], d_plus),
        (tab.at[1, spot(zh, x + 1), core], tab.at[1, spot(zh, x + 2), core], d_minus),
        (tab.at[0, spot(nh, x - 1), core], tab.at[0, spot(nh, x + 2), core], d_plus),
        (tab.at[1, spot(nh, x + 1), core], tab.at[1, spot(nh, x + 2), core], d_minus),
        (line(zh, core), line(zh, 1 - core), d_core),
        (line(nh, core), line(nh, 1 - core), d_core),
    ]

    def p_go(*which):
        for m in which:
            block, _, target = prompts[m]
            send(block, block, p_send.at[m], p_recv.at[m], "dp", target)

    def p_wait(*which):
        for m in which:
            landed(prompts[m][1], p_recv.at[m])

    def spread(block, landing, ss, rs):
        for k in range(1, N_DP):
            peer = lax.rem(dp + k, N_DP)
            send(block(peer), landing, ss, rs, "dp", peer)
        pltpu.make_async_copy(block(dp), landing, rs).start()

    h_send(0, 0)
    p_go(0, 1, 2)
    h_send(1, 0)
    p_wait(1, 2)
    p_go(5, 6)
    p_wait(0)
    p_go(3, 4)
    h_wait(0, 0)
    h_send(0, 1)
    h_send(2, 0, (0, 3))
    h_wait(1, 0)
    p_wait(3, 4)
    p_go(7, 8)
    p_wait(5, 6)
    p_go(9)
    h_wait(0, 1)
    h_send(0, 2)
    h_send(1, 1)
    h_send(2, 0, (3, 6))
    h_send(3, 0, (0, 3))
    p_wait(7, 8)
    p_go(10)
    for one in mine[3:]:
        one.wait()
    p_wait(9, 10)


    by_row = tab[0, :, :, PROMPT:].astype(f32)[:, :, 0:8].reshape(128, 128)
    by_lane = by_row.T
    i_row = lax.broadcasted_iota(jnp.int32, (128, 128), 0)
    i_lane = lax.broadcasted_iota(jnp.int32, (128, 128), 1)
    before = jnp.where((by_row == by_lane) & (i_row < i_lane), 1.0, 0.0)
    rank = jnp.sum(before, 0, keepdims=True)
    rank = jnp.broadcast_to(4.0 * by_lane[0:1] + rank, (64, 128))
    number = (lax.shift_right_logical(i_lane, 3) * RESP + (i_lane & 7)).astype(f32)
    hit = jnp.where(rank == i_row[:64].astype(f32), number[:64], 0.0)
    index = jnp.sum(hit, 1, keepdims=True)
    idx_v[...] = jnp.broadcast_to(index, (64, 128)).astype(jnp.int32)
    to_s = pltpu.make_async_copy(idx_v, idx_s, lsem.at[0])
    to_s.start()

    key_at = lax.broadcasted_iota(jnp.int32, (LEN, WIDE), 0)
    row_at = lax.rem(lax.broadcasted_iota(jnp.int32, (LEN, WIDE), 1), LEN)
    causal = key_at <= row_at
    t_at = lax.broadcasted_iota(jnp.int32, (HEADS_DEV * HD, LEN), 1)

    def give(c, i):
        spread(lambda k: ctr.at[c, i, k], (rbk, rbv)[i].at[c, dp], a_send.at[c, i], a_recv.at[c, i])

    def add_up(i):
        for c in range(RESP):
            landed((rbk, rbv)[i].at[c], a_recv.at[c, i])

        @pl.loop(1, N_DP + 1)
        def _(n):
            s = lax.rem(dp + n, N_DP)
            total = jnp.zeros((PIECE, HD), f32)
            for k in range(RESP):
                r = idx_s[s * RESP + k, 0]
                total += (rbk, rbv)[i][r & (RESP - 1), lax.shift_right_logical(r, 2) & (N_DP - 1)].astype(f32)
            fin[i, s] = total.astype(bf16)
            landing = (dpk, dpv)[i].at[pl.ds(pl.multiple_of(dp * PIECE, PIECE), PIECE)]

            @pl.when(n < N_DP)
            def _():
                send(fin.at[i, s], landing, f_send.at[i], f_recv.at[i], "dp", s)

            @pl.when(n == N_DP)
            def _():
                pltpu.make_async_copy(fin.at[i, s], landing, f_recv.at[i]).start()

    def rows_of(c):
        return pl.ds(pl.multiple_of(c * LEN, LEN), LEN)

    def heads(ref, c, h):
        return jnp.concatenate(
            [ref[rows_of(c), pl.ds(pl.multiple_of((h * HPI + i) * HD, HD), HD)] for i in range(HPI)], 0
        )

    def load_keys(c):
        slot = owner_ref[group_ref[c]]
        spot_slot = lax.shift_right_logical(slot, 1) & 7
        ka[0:PROMPT] = tab[0, spot_slot, slot & 1, 0:PROMPT]
        va[0:PROMPT] = tab[1, spot_slot, slot & 1, 0:PROMPT]
        ka[PROMPT:KEYS] = ko[rows_of(c)]
        va[PROMPT:KEYS] = vo[rows_of(c)]
        kt[...] = ka[...].astype(f32).T.astype(bf16)

    def probs(c, h):
        s = dotf(ka[...], heads(q, c, h), NT)
        so = jnp.where(causal, s[PROMPT:], -jnp.inf)
        sp = s[:PROMPT]
        m = jnp.maximum(jnp.max(sp, 0, keepdims=True), jnp.max(so, 0, keepdims=True))
        ep = jnp.exp2((sp - m) * SCALE_LOG2E)
        eo = jnp.exp2((so - m) * SCALE_LOG2E)
        inv = 1.0 / (jnp.sum(ep, 0, keepdims=True) + jnp.sum(eo, 0, keepdims=True))
        return jnp.concatenate([ep * inv, eo * inv], 0)

    def dscore(c, h, p, pr):
        d = dotf(va[...], heads(g, c, h), NT)
        delta = jnp.sum(pr.astype(f32) * d, 0, keepdims=True)
        return (p * (d - delta)).astype(bf16)

    def query_grad(c, h, ds):
        dqt = dotf(kt[...], ds) * SCALE
        for i in range(HPI):
            head = pl.ds(pl.multiple_of((h * HPI + i) * HD, HD), HD)
            dq[rows_of(c), head] = dqt[:, i * LEN : (i + 1) * LEN].T.astype(bf16)

    def shards(c, *which):
        return sum(dotf(w[:, cols(t_)], dh[rows_of(c), cols(t_)], NT) for t_ in which)

    def grad_rows(c, grad):
        g[rows_of(c), :] = jnp.where(t_at < length_ref[c], grad, 0.0).T.astype(bf16)

    def pieces(c, i, total):
        ctr[c, i] = total.astype(bf16).reshape(N_DP, PIECE, HD)
        give(c, i)

    def results(c):
        rows = rows_of(c)
        dko[rows] = (dka[PROMPT:KEYS] * SCALE).astype(bf16)
        dvo[rows] = dva[PROMPT:KEYS].astype(bf16)

    final = RESP - 1
    @pl.loop(0, final)
    def _(c):
        load_keys(c)
        dka[...] = jnp.zeros_like(dka)
        dva[...] = jnp.zeros_like(dva)
        h_wait(c, 2)
        grad_rows(c, dotf(w[...], dh[rows_of(c), :], NT))

        @pl.loop(0, HALVES)
        def _(h):
            p = probs(c, h)
            pr = p.astype(bf16)
            ds = dscore(c, h, p, pr)
            dva[...] += dotf(pr, heads(g, c, h))
            dka[...] += dotf(ds, heads(q, c, h))
            query_grad(c, h, ds)

            @pl.when(h == 0)
            def _():
                h_wait(c + 1, 1)
                h_send(c + 1, 2)

        @pl.when(c <= 1)
        def _():
            h_wait(c + 2, 0)
            h_send(c + 2, 1)

        @pl.when(c == 0)
        def _():
            h_send(final, 0, (3, 6))

        pieces(c, 1, dva[0:PROMPT])
        pieces(c, 0, dka[0:PROMPT] * SCALE)
        results(c)

        @pl.when(c == 0)
        def _():
            load_keys(final)

            @pl.loop(0, HALVES)
            def _(h):
                p = probs(final, h)
                pb[h] = p
                prb[h] = p.astype(bf16)

        @pl.when(c == 1)
        def _():
            gacc[...] = shards(final, ten, t_plus, t_minus, t_z)

    gacc[...] += shards(final, far(zl, y + 2), far(nz, y - 1), far(nz, y + 1))
    load_keys(final)
    dka[...] = jnp.zeros_like(dka)
    dva[...] = jnp.zeros_like(dva)
    h_wait(final, 2)
    grad_rows(final, gacc[...] + shards(final, far(nz, y + 2)))

    @pl.loop(0, HALVES)
    def _(h):
        dva[...] += dotf(prb[h], heads(g, final, h))

    pieces(final, 1, dva[0:PROMPT])

    @pl.loop(0, HALVES)
    def _(h):
        ds = dscore(final, h, pb[h], prb[h])
        dsb[h] = ds
        dka[...] += dotf(ds, heads(q, final, h))

    pieces(final, 0, dka[0:PROMPT] * SCALE)
    to_s.wait()
    add_up(1)

    @pl.loop(0, HALVES)
    def _(h):
        query_grad(final, h, dsb[h])

    results(final)
    add_up(0)
    for c in range(RESP):
        h_done(c)
        for i in range(2):
            landed(ctr.at[c, i, 0:15], a_send.at[c, i])
    for m, (block, _, _) in enumerate(prompts):
        landed(block, p_send.at[m])
    for i, out in ((1, dpv), (0, dpk)):
        landed(out, f_recv.at[i])
    for i in range(2):
        landed(fin.at[i, 0:15], f_send.at[i])


def hand_over(*refs):
    n = len(refs) // 2
    copies = [pltpu.make_async_copy(refs[i], refs[n + i], refs[-1].at[i]) for i in range(n)]
    for one in copies:
        one.start()
    for one in copies:
        one.wait()


def body(q, k, v, h, w, pk, pv, group, length, owner):
    def out(a):
        return jax.ShapeDtypeStruct(a.shape, a.dtype)

    any_, vmem, smem = (pl.BlockSpec(memory_space=m) for m in (pl.ANY, pltpu.VMEM, pltpu.SMEM))
    dma = pltpu.SemaphoreType.DMA
    outs = (out(q), out(k), out(v), out(pk), out(pv))
    grads = pl.pallas_call(
        kernel,
        out_shape=tuple(pltpu.VMEM(a.shape, a.dtype) for a in outs),
        in_specs=[smem] * 3 + [any_] * 7,
        out_specs=(vmem,) * 5,
        scratch_shapes=[
            pltpu.VMEM((RESP * LEN, 8 * SHARD), bf16),
            pltpu.VMEM((HEADS_DEV * HD, 8 * SHARD), bf16),
            pltpu.VMEM((RESP * LEN, HEADS_DEV * HD), bf16),
            pltpu.VMEM((RESP * LEN, HEADS_DEV * HD), bf16),
            pltpu.VMEM((RESP * LEN, HD), bf16),
            pltpu.VMEM((RESP * LEN, HD), bf16),
            pltpu.VMEM((2, 8, 2, PROMPT + EXTRA, HD), bf16),
            pltpu.VMEM((KEYS, HD), bf16),
            pltpu.VMEM((KEYS, HD), bf16),
            pltpu.VMEM((HD, KEYS), bf16),
            pltpu.VMEM((HEADS_DEV * HD, LEN), f32),
            pltpu.VMEM((HALVES, KEYS, WIDE), f32),
            pltpu.VMEM((HALVES, KEYS, WIDE), bf16),
            pltpu.VMEM((HALVES, KEYS, WIDE), bf16),
            pltpu.VMEM((KEYS, HD), f32),
            pltpu.VMEM((KEYS, HD), f32),
            pltpu.VMEM((RESP, 2, N_DP, PIECE, HD), bf16),
            pltpu.VMEM((RESP, N_DP, PIECE, HD), bf16),
            pltpu.VMEM((RESP, N_DP, PIECE, HD), bf16),
            pltpu.VMEM((2, N_DP, PIECE, HD), bf16),
            pltpu.VMEM((64, 128), jnp.int32),
            pltpu.SMEM((64, 128), jnp.int32),
            dma((7,)), dma((RESP, 17)), dma((RESP, 17)), dma((11,)), dma((11,)),
            dma((RESP, 2)), dma((RESP, 2)), dma((2,)), dma((2,)),
        ],
        compiler_params=pltpu.CompilerParams(
            collective_id=0, has_side_effects=True, vmem_limit_bytes=56 * 2**20
        ),
        cost_estimate=pl.CostEstimate(flops=19 * 10**9, bytes_accessed=20 * 10**6, transcendentals=6 * 10**6),
        name="attention_backward",
    )(group, length, owner, q, k, v, h, w, pk, pv)
    return pl.pallas_call(
        hand_over,
        out_shape=outs,
        in_specs=[vmem] * 5,
        out_specs=(any_,) * 5,
        scratch_shapes=[dma((5,))],
        compiler_params=pltpu.CompilerParams(vmem_limit_bytes=4 * 2**20),
        name="hand_over",
    )(*(pltpu.with_memory_space_constraint(a, pltpu.VMEM) for a in grads))


def solution(mesh):
    whole = P("dp", "tensor")
    return jax.shard_map(
        body,
        mesh=mesh,
        in_specs=(whole, whole, whole, whole, P("tensor", None), whole, whole, P("dp"), P("dp"), P()),
        out_specs=(whole,) * 5,
        check_vma=False,
    )
```
